128 devices in a mesh: grid: 16 (over x, z), mode: 8 (over y, core).
Axes of the slice: x: 4, y: 4, z: 4, core: 2. Of those that a mesh axis runs over, the one named last changes fastest.
Arguments:
- state: bfloat16 [2, 1024, 64, 4096], P(None, 'mode', 'grid'), may hold values from 0.049804688 to 2
- film_mask: int32 [64, 4096], P('grid'), may hold values 0 or 1
- basis: bfloat16 [2, 256, 64, 4096], P(None, 'mode', 'grid'), may hold values from -0.0078125 to 0.0078125
- sample_cells: int32 [16, 512], P('grid'), may hold values from 0 to 16383
- owner: int32 [16, 512, 1], P('grid'), may hold values from 0 to 127; in each aligned block of 512 rows (0 to 511, 512 to 1023, ..., all dimensions but the last counted through in order) at most 8 rows name the same one
Outputs:
- reduced_proj: float32 [256, 1024], P('grid', 'mode')
- sampled: bfloat16 [128, 128, 2560], P(('grid', 'mode'))
- hyper_gram: float32 [256, 256], P(('grid', 'mode'))
- hyper_proj: float32 [256, 1024], P(('grid', 'mode'))
The draws below stay inside these ranges and needn't reach their ends.
Inputs may be any that keep to these rules, and one draw needn't show every extreme that they name: Among the 512 samples of one grid block, at most 8 share an owner.
All inputs are finite; a program needn't handle non-finite values. No bound on the sum of `film_mask` on one device may be relied on, other than what follows from the above.
Results may differ from the reference program's by a relative error of at most 0.0029.
Values may be sent and summed in bfloat16 or wider, within the bound.
A program may use at most 128 MiB of HBM per device.

```python
import math
import jax
import jax.numpy as jnp
import numpy as np

NCOL = 4096
K = 256
SAMP = 512
NROWS = 64
NS = 1024
CELLS_DEV = 16384
CAP = 8
N_GRID = 16
DEVICES = 128


def touch_ends(entries, stream_key, low, largest):
    shape = entries.shape
    index_at = [jax.random.randint(jax.random.fold_in(stream_key, axis), (), 0, shape[axis]) for axis in range(len(shape))]
    entries = entries.at[tuple(index_at)].set(low)
    longest = shape.index(max(shape))
    index_at[longest] = (index_at[longest] + 1) % shape[longest]
    return entries.at[tuple(index_at)].set(largest)


def steps_of(key, extent, cuts, least, top_value):
    factor_of = 1.0
    for dim, blocks in cuts:
        heights = jax.random.uniform(jax.random.fold_in(jax.random.fold_in(key, 6), dim), (blocks,), jnp.float32, least / len(cuts), top_value / len(cuts))
        factor_of = factor_of * jnp.repeat(jnp.exp(heights), extent[dim] // blocks).reshape((-1,) + (1,) * (len(extent) - 1 - dim))
    return factor_of


def routed_block(key, own, number, rows, count, top, bound, slope):
    ranking = jax.random.permutation(key, count)
    crowded, common = shares(count, rows * top, bound, slope, True), shares(count, rows * top, bound, slope, False)
    places = jnp.arange(count)

    def named(sizes, turn):
        used = int((sizes > 0).sum())
        fixed = max(1, used // 4)
        moved = fixed + (places - fixed + turn * (used - fixed)) % max(1, count - fixed)
        return jnp.zeros((count,), jnp.int32).at[ranking[jnp.where(places < fixed, places, moved)]].set(jnp.asarray(sizes, jnp.int32))

    sizes = jnp.where(number % 4 == 0, named(crowded, number // 4), named(common, number - number // 4 - 1))
    mixed = jax.random.permutation(jax.random.fold_in(own, 3), count)
    source_of, taker = mixed[0:count // 2 * 2:2], mixed[1:count // 2 * 2:2]
    slack = jnp.minimum(sizes[source_of] - 1, bound - sizes[taker]) // 2
    slack = jnp.where((source_of == ranking[0]) | (taker == ranking[0]) | (sizes[taker] == 0), 0, jnp.maximum(slack, 0))
    moved = jax.random.randint(jax.random.fold_in(own, 4), (count // 2,), 0, 1 << 20) % (slack + 1)
    sizes = sizes.at[source_of].add(-moved).at[taker].add(moved)
    items = jnp.searchsorted(jnp.cumsum(sizes), jnp.arange(rows * top), side="right").astype(jnp.int32)
    table = items.reshape(top, rows).T
    table = table[jax.random.permutation(jax.random.fold_in(own, 1), rows)]
    turn = jax.random.randint(jax.random.fold_in(own, 2), (rows, 1), 0, top)
    return jnp.take_along_axis(table, (jnp.arange(top)[None, :] + turn) % top, axis=1)


def shares(amount, total, bound, slope, full):
    portions = [(1 << 20) // math.isqrt(rank ** slope) + 1 for rank in range(1, amount + 1)]
    largest = bound if full else min(bound, max(-(-total // amount), total * portions[0] // sum(portions)))
    least = 1 if total - largest >= amount - 1 else 0
    holding, spare = [largest] + [least] * (amount - 1), total - largest - least * (amount - 1)
    while spare > 0:
        free = [i for i in range(1, amount) if holding[i] < largest] or [i for i in range(1, amount) if holding[i] < bound]
        pool, remaining = sum([portions[i] for i in free]), spare
        for i in free:
            extra = min(bound - holding[i], max(1, remaining * portions[i] // pool), spare)
            holding[i] = holding[i] + extra
            spare = spare - extra
    return np.array(holding)


def centred(own_key, extent, width, most, cuts=(), held_as=jnp.bfloat16):
    entries = width * jax.random.normal(own_key, extent, jnp.float32)
    if cuts:
        entries = entries * steps_of(own_key, extent, cuts, -0.22, 0.18)
    return jnp.clip(entries, -most, most).astype(held_as)


def setup_inputs(seed: int = 0) -> dict:
    splits = jax.random.split(jax.random.key(seed), 6)
    state = jnp.clip(0.049804688 + 1.9501953 * jax.random.uniform(splits[0], (2, NS, NROWS, NCOL), jnp.float32) ** steps_of(splits[0], (2, NS, NROWS, NCOL), ((1, 8), (2, 16)), -0.2, 0.2), 0.049804688, 2.0).astype(jnp.bfloat16)
    film_mask = touch_ends((jax.random.randint(splits[1], (NROWS, NCOL), 0, 5) < 3).astype(jnp.int32), jax.random.fold_in(splits[1], 1), 0, 1)
    basis = centred(splits[2], (2, K, NROWS, NCOL), (2 * NROWS * NCOL) ** -0.5, 0.0078125, ((1, 8), (2, 16)))
    sample_cells = touch_ends(jax.random.randint(splits[3], (N_GRID, SAMP), 0, CELLS_DEV), jax.random.fold_in(splits[3], 1), 0, CELLS_DEV - 1).astype(jnp.int32)
    owner_keys = jax.random.split(jax.random.fold_in(splits[4], 1), N_GRID * SAMP // SAMP)
    owner_turns = jax.random.permutation(jax.random.fold_in(splits[4], 3), N_GRID * SAMP // SAMP)
    owner = jax.vmap(lambda own, number: routed_block(jax.random.fold_in(splits[4], 2), own, number, SAMP, DEVICES, 1, CAP, 2))(owner_keys, owner_turns).reshape((N_GRID, SAMP, 1))
    return {"state": state, "film_mask": film_mask, "basis": basis, "sample_cells": sample_cells, "owner": owner}


def rates_of(state, film_mask):
    substrate = state[0].astype(jnp.float32)
    biomass = state[1].astype(jnp.float32)
    biofilm = film_mask.astype(jnp.float32)
    padded = jnp.pad(substrate, ((0, 0), (1, 1), (1, 1)))
    laplace = padded[:, 2:, 1:-1] + padded[:, :-2, 1:-1] + padded[:, 1:-1, 2:] + padded[:, 1:-1, :-2] - 4.0 * substrate
    uptake = substrate / (0.5 + substrate)
    sub_rate = (1.0 - 0.2 * biofilm) * laplace - 2.0 * biomass * uptake
    bio_rate = biofilm * (biomass * uptake - 0.1 * biomass)
    return jnp.stack([sub_rate, bio_rate]).astype(jnp.bfloat16)


def reference(state, film_mask, basis, sample_cells, owner):
    rate = rates_of(state, film_mask)
    basis_flat = basis.reshape(2, K, -1)
    rate_flat = rate.reshape(2, NS, -1)
    reduced_proj = jnp.zeros((K, NS), jnp.float32)
    for species in range(2):
        reduced_proj = reduced_proj + jnp.dot(basis_flat[species], rate_flat[species].T, preferred_element_type=jnp.float32)
    global_cells = (jnp.arange(N_GRID, dtype=jnp.int32)[:, None] * CELLS_DEV + sample_cells).reshape(-1).astype(jnp.int32)
    picked_basis = jnp.take(basis_flat, global_cells, axis=2)
    picked_rate = jnp.take(rate_flat, global_cells, axis=2)
    weight_rows = CELLS_DEV / SAMP
    hyper_gram = jnp.zeros((K, K), jnp.float32)
    hyper_proj = jnp.zeros((K, NS), jnp.float32)
    for species in range(2):
        hyper_gram = hyper_gram + jnp.dot(picked_basis[species], picked_basis[species].T, preferred_element_type=jnp.float32)
        hyper_proj = hyper_proj + jnp.dot(picked_basis[species], picked_rate[species].T, preferred_element_type=jnp.float32)
    hyper_gram = weight_rows * hyper_gram
    hyper_proj = weight_rows * hyper_proj
    owners = owner[:, :, 0]
    onehot = (owners[:, :, None] == jnp.arange(DEVICES, dtype=jnp.int32)[None, None, :]).astype(jnp.int32)
    slot_rank = jnp.sum((jnp.cumsum(onehot, axis=1) - 1) * onehot, axis=2)
    slots = (jnp.arange(N_GRID, dtype=jnp.int32)[:, None] * CAP + slot_rank).reshape(-1).astype(jnp.int32)
    total = N_GRID * SAMP
    rows = jnp.concatenate([picked_basis.transpose(2, 0, 1).reshape(total, 2 * K), picked_rate.transpose(2, 0, 1).reshape(total, 2 * NS)], axis=1)
    sampled = jnp.zeros((DEVICES, N_GRID * CAP, 2 * K + 2 * NS), jnp.bfloat16)
    sampled = sampled.at[owners.reshape(-1).astype(jnp.int32), slots].set(rows)
    return reduced_proj, sampled, hyper_gram, hyper_proj
```

```python
import functools

import jax
import jax.numpy as jnp
from jax import lax
from jax.experimental import pallas as pl
from jax.experimental.pallas import tpu as pltpu
from jax.sharding import PartitionSpec as P

MESH = pl.DeviceIdType.MESH
F32 = jnp.float32
BF16 = jnp.bfloat16


def dot_nt(a, b):
    return lax.dot_general(a, b, (((1,), (1,)), ((), ())), preferred_element_type=F32)


def kernel(
    ng, nm, weight,
    state, basis, mask, cell_row, own_row,
    o_red, o_samp, o_gram, o_proj,
    raw_b, raw_s, st, rate, gat, hot, cellb, slots,
    acc_p, acc_b, picks, pbg, t1, t1r, w32, w16, w16r, hb, hr, mb, mr, fb, fr,
    lsem, ssem, rsem, hsem, psem, tsem, wsem, qsem, msem, fsem,
):
    g = lax.axis_index("grid")
    m = lax.axis_index("mode")
    ny = nm // 2
    c = lax.rem(m, 2)
    y = m // 2
    right = lax.rem(y + 1, ny) * 2 + c
    left = lax.rem(y + ny - 1, ny) * 2 + c
    opp = lax.rem(y + 2, ny) * 2 + c
    sib = y * 2 + (1 - c)
    flip = 1 - 2 * c
    modes = basis.shape[1]
    snaps = state.shape[1]
    nrow = state.shape[2]
    ncol = state.shape[3]
    samp = cell_row.shape[1]
    nchunk = 2 * nrow

    loads = []
    for s in range(2):
        loads.append(pltpu.make_async_copy(basis.at[s], raw_b.at[s], lsem.at[s]))
    for s in range(2):
        loads.append(pltpu.make_async_copy(state.at[s], raw_s.at[s], lsem.at[2 + s]))
    for load in loads:
        load.start()

    barrier = pltpu.get_barrier_semaphore()
    for d in range(1, nm):
        pl.semaphore_signal(barrier, inc=1, device_id=(g, lax.rem(m + d, nm)), device_id_type=MESH)
    for d in range(1, ng):
        pl.semaphore_signal(barrier, inc=1, device_id=(lax.rem(g + d, ng), m), device_id_type=MESH)
    pl.semaphore_wait(barrier, nm - 1 + ng - 1)

    sent = []

    def push(src, dst, send_sem, recv_sem, device):
        copy = pltpu.make_async_remote_copy(
            src_ref=src, dst_ref=dst, send_sem=send_sem, recv_sem=recv_sem,
            device_id=device, device_id_type=MESH,
        )
        copy.start()
        sent.append(copy)

    def await_recv(dst, send_sem, recv_sem):
        pltpu.make_async_remote_copy(
            src_ref=dst, dst_ref=dst, send_sem=send_sem, recv_sem=recv_sem,
            device_id=(g, sib), device_id_type=MESH,
        ).wait_recv()

    def ag_send(owner, j, kind, to):
        push(gat.at[j, owner], gat.at[j, owner], ssem.at[kind, j], rsem.at[owner, j], (g, to))

    def ag_recv(owner, j):
        await_recv(gat.at[j, owner], ssem.at[0, j], rsem.at[owner, j])

    def serve(j):
        ag_recv(left, j)
        if j % 2 == 0:
            ag_send(left, j, 3, right)
        ag_send(left, j, 4, sib)
        ag_recv(right, j)
        if j % 2 == 1:
            ag_send(right, j, 3, left)
        ag_send(right, j, 5, sib)

    for s in range(2):
        loads[s].wait()
        gat[pl.ds(s * nrow, nrow), m] = jnp.swapaxes(raw_b[s], 0, 1)
        for j in range(s * nrow, (s + 1) * nrow):
            ag_send(m, j, 0, right)
            ag_send(m, j, 1, left)
            ag_send(m, j, 2, sib)

    step = 16
    loads[2].wait()

    def split_s(i, carry):
        rows = pl.ds(pl.multiple_of(i * step, step), step)
        st[pl.ds(1, nrow), rows] = jnp.swapaxes(raw_s[0, rows], 0, 1)
        return carry

    lax.fori_loop(0, snaps // step, split_s, 0)
    up_dev = lax.rem(g + 1, ng)
    down_dev = lax.rem(g + ng - 1, ng)
    push(st.at[nrow], st.at[0], hsem.at[0], hsem.at[1], (up_dev, m))
    push(st.at[1], st.at[nrow + 1], hsem.at[2], hsem.at[3], (down_dev, m))
    loads[3].wait()

    def split_b(i, carry):
        rows = pl.ds(pl.multiple_of(i * step, step), step)
        high = pl.ds(pl.multiple_of(i * step + snaps, step), step)
        rate[:, high] = jnp.swapaxes(raw_s[1, rows], 0, 1)
        return carry

    lax.fori_loop(0, snaps // step, split_b, 0)

    lane = lax.broadcasted_iota(jnp.int32, (step, ncol), 1)

    def rates(r):
        film = jnp.broadcast_to(mask[pl.ds(r, 1), :].astype(F32), (step, ncol))
        up_on = jnp.where(jnp.logical_and(r == 0, g == 0), 0.0, 1.0).astype(F32)
        down_on = jnp.where(jnp.logical_and(r == nrow - 1, g == ng - 1), 0.0, 1.0).astype(F32)

        def body(i, carry):
            rows = pl.ds(pl.multiple_of(i * step, step), step)
            high = pl.ds(pl.multiple_of(i * step + snaps, step), step)
            sub = st[r + 1, rows].astype(F32)
            up = st[r, rows].astype(F32) * up_on
            down = st[r + 2, rows].astype(F32) * down_on
            bio = rate[r, high].astype(F32)
            before = jnp.where(lane == 0, 0.0, pltpu.roll(sub, 1, 1))
            after = jnp.where(lane == ncol - 1, 0.0, pltpu.roll(sub, ncol - 1, 1))
            lap = down + up + after + before - 4.0 * sub
            taken = bio * (sub / (0.5 + sub))
            rate[r, rows] = ((1.0 - 0.2 * film) * lap - 2.0 * taken).astype(BF16)
            rate[r, high] = (film * (taken - 0.1 * bio)).astype(BF16)
            return carry

        lax.fori_loop(0, snaps // step, body, 0)

    for r in range(1, nrow - 1):
        rates(r)
    serve(0)
    await_recv(st.at[0], hsem.at[0], hsem.at[1])
    await_recv(st.at[nrow + 1], hsem.at[2], hsem.at[3])
    rates(0)
    serve(1)
    rates(nrow - 1)
    serve(2)

    ii = lax.broadcasted_iota(jnp.int32, (samp, samp), 0)
    jj = lax.broadcasted_iota(jnp.int32, (samp, samp), 1)
    own = jnp.broadcast_to(own_row[...].astype(F32), (samp, samp))
    cel = jnp.broadcast_to(cell_row[...].astype(F32), (samp, samp))
    cell_col = jnp.sum(jnp.where(ii == jj, cel, 0.0), axis=1, keepdims=True)
    own_col = jnp.sum(jnp.where(ii == jj, own, 0.0), axis=1, keepdims=True)
    cellb[...] = jnp.broadcast_to(cell_col, cellb.shape)
    same = jnp.logical_and(own == own_col, ii < jj)
    rank = jnp.sum(jnp.where(same, 1.0, 0.0), axis=0, keepdims=True)
    own_f = own_row[...].astype(F32)
    own_hi = jnp.floor(own_f * (1.0 / nm))
    key = (own_f - own_hi * nm) * 128.0 + own_hi * 8.0 + rank
    for mm in range(nm):
        number = lax.broadcasted_iota(jnp.int32, (128, samp), 0).astype(F32) + float(mm * 128)
        slots[mm] = jnp.where(number == key, 1.0, 0.0).astype(BF16)

    lanes = lax.broadcasted_iota(jnp.int32, (samp, 128), 1).astype(F32)
    for r in range(nrow):
        def build(i, carry):
            base = (r * ncol + i * 128).astype(F32)
            cols = pl.ds(pl.multiple_of(i * 128, 128), 128)
            hot[:, cols] = jnp.where(cellb[...] == lanes + base, 1.0, 0.0).astype(BF16)
            return carry

        lax.fori_loop(0, ncol // 128, build, 0)
        part = dot_nt(rate[r], hot[...])
        acc_p[...] = part if r == 0 else acc_p[...] + part
        for s in range(2):
            part = dot_nt(gat[s * nrow + r, m], hot[...])
            acc_b[s] = part if r == 0 else acc_b[s] + part
        serve(3 + r)
    picks[...] = acc_p[...].astype(BF16)
    pbg[m] = acc_b[...].astype(BF16)
    for d in range(1, nm):
        to = lax.rem(m + d, nm)
        push(pbg.at[m], pbg.at[m], psem.at[0, d], psem.at[1, d], (g, to))
    for mm in range(nm):
        t1[mm] = dot_nt(slots[mm], picks[...]).astype(BF16)
    t1r[m] = t1[m]
    for d in range(1, nm):
        to = lax.rem(m + d, nm)
        push(t1.at[to], t1r.at[m], tsem.at[0, d], tsem.at[1, d], (g, to))
    serve(nchunk - 1)

    for d in range(1, nm):
        frm = lax.rem(m + nm - d, nm)
        await_recv(pbg.at[frm], psem.at[0, d], psem.at[1, d])

    hyper = jnp.zeros((nm * modes, snaps), F32)
    gram = jnp.zeros((nm * modes, modes), F32)
    for s in range(2):
        all_modes = pbg[:, s].reshape(nm * modes, samp)
        hyper = hyper + dot_nt(all_modes, picks[s * snaps : (s + 1) * snaps, :])
        gram = gram + dot_nt(all_modes, pbg[m, s])
        w32[:, 0:8, s * 256 : (s + 1) * 256] = dot_nt(slots[m], all_modes).reshape(ng, 8, nm * modes)
    hb[...] = jnp.zeros(hb.shape, F32)
    hb[:, :, 0:128] = (weight * hyper).reshape(ng, 16, snaps)
    hb[:, :, 128 : 128 + modes] = (weight * gram).reshape(ng, 16, modes)
    for d in range(1, ng):
        to = lax.rem(g + d, ng)
        push(hb.at[to], hr.at[g], qsem.at[0, d], qsem.at[1, d], (to, m))
    hr[g] = hb[g]

    for d in range(1, nm):
        frm = lax.rem(m + nm - d, nm)
        await_recv(t1r.at[frm], tsem.at[0, d], tsem.at[1, d])
    half = w32.shape[2]
    for mm in range(nm):
        for s in range(2):
            col = 2 * nm * modes + s * nm * snaps + mm * snaps
            block = t1r[mm, :, s * snaps : (s + 1) * snaps].astype(F32).reshape(ng, 8, snaps)
            if col < half:
                w32[:, 0:8, col : col + snaps] = block
            else:
                w32[:, 8:16, col - half : col - half + snaps] = block
    w16[...] = w32[...].astype(BF16)
    for d in range(1, ng):
        to = lax.rem(g + d, ng)
        push(w16.at[to], w16r.at[g], wsem.at[0, d], wsem.at[1, d], (to, m))
    w16r[g] = w16[g]

    for j in range(nchunk // 2):
        ag_recv(opp, j)
        ag_send(opp, j, 6, sib)

    for d in range(1, ng):
        frm = lax.rem(g + ng - d, ng)
        await_recv(hr.at[frm], qsem.at[0, d], qsem.at[1, d])
    total = jnp.sum(hr[...], axis=0)
    mb[...] = jnp.zeros(mb.shape, F32)
    for mm in range(nm):
        mb[mm, 0:2, :] = total[2 * mm : 2 * mm + 2, :]
    for d in range(1, nm):
        to = lax.rem(m + d, nm)
        push(mb.at[to], mr.at[m], msem.at[0, d], msem.at[1, d], (g, to))
    mr[m] = mb[m]

    fb[...] = jnp.zeros(fb.shape, F32)

    def project(j):
        s, r = j // nrow, j % nrow
        for owner in (sib, right + flip, left + flip, opp + flip):
            ag_recv(owner, j)
        block = gat[j].reshape(nm * modes, ncol)
        part = dot_nt(block, rate[r, s * snaps : (s + 1) * snaps, :])
        fb[...] += part.reshape(fb.shape)

    for j in range(nchunk // 2):
        project(j)
    for d in range(1, ng):
        frm = lax.rem(g + ng - d, ng)
        await_recv(w16r.at[frm], wsem.at[0, d], wsem.at[1, d])
    for h in range(2):
        part = w16r[...].astype(F32)[:, 8 * h : 8 * h + 8, :].reshape(ng * 8, half)
        o_samp[0, :, h * half : (h + 1) * half] = part.astype(BF16)
    for d in range(1, nm):
        frm = lax.rem(m + nm - d, nm)
        await_recv(mr.at[frm], msem.at[0, d], msem.at[1, d])
    for mm in range(nm):
        o_proj[:, mm * snaps : (mm + 1) * snaps] = mr[mm, 0:2, 0:snaps]
        o_gram[:, mm * modes : (mm + 1) * modes] = mr[mm, 0:2, 128 : 128 + modes]
    for j in range(nchunk // 2, nchunk):
        ag_recv(opp, j)
        ag_send(opp, j, 6, sib)
    for j in range(nchunk // 2, nchunk):
        project(j)

    for d in range(1, ng):
        to = lax.rem(g + d, ng)
        push(fb.at[to], fr.at[g], fsem.at[0, d], fsem.at[1, d], (to, m))
    fr[g] = fb[g]
    for d in range(1, ng):
        frm = lax.rem(g + ng - d, ng)
        await_recv(fr.at[frm], fsem.at[0, d], fsem.at[1, d])
    o_red[...] = jnp.sum(fr[...], axis=0)
    for copy in sent:
        copy.wait_send()


def per_device(ng, nm, state, film_mask, basis, sample_cells, owner):
    modes, snaps = basis.shape[1], state.shape[1]
    nrow, ncol = state.shape[2:]
    samp = sample_cells.shape[1]
    nchunk = 2 * nrow
    width = 2 * nm * (modes + snaps)
    dma = pltpu.SemaphoreType.DMA
    vmem = pl.BlockSpec(memory_space=pltpu.VMEM)
    hbm = pl.BlockSpec(memory_space=pl.ANY)
    return pl.pallas_call(
        functools.partial(kernel, ng, nm, nrow * ncol / samp),
        out_shape=(
            jax.ShapeDtypeStruct((nm * modes // ng, snaps), F32),
            jax.ShapeDtypeStruct((1, ng * 8, width), BF16),
            jax.ShapeDtypeStruct((2, nm * modes), F32),
            jax.ShapeDtypeStruct((2, nm * snaps), F32),
        ),
        in_specs=[hbm, hbm, vmem, vmem, vmem],
        out_specs=(vmem, vmem, vmem, vmem),
        scratch_shapes=[
            pltpu.VMEM((2, modes, nrow, ncol), BF16),
            pltpu.VMEM((2, snaps, nrow, ncol), BF16),
            pltpu.VMEM((nrow + 2, snaps, ncol), BF16),
            pltpu.VMEM((nrow, 2 * snaps, ncol), BF16),
            pltpu.VMEM((nchunk, nm, modes, ncol), BF16),
            pltpu.VMEM((samp, ncol), BF16),
            pltpu.VMEM((samp, 128), F32),
            pltpu.VMEM((nm, 128, samp), BF16),
            pltpu.VMEM((2 * snaps, samp), F32),
            pltpu.VMEM((2, modes, samp), F32),
            pltpu.VMEM((2 * snaps, samp), BF16),
            pltpu.VMEM((nm, 2, modes, samp), BF16),
            pltpu.VMEM((nm, 128, 2 * snaps), BF16),
            pltpu.VMEM((nm, 128, 2 * snaps), BF16),
            pltpu.VMEM((ng, 16, width // 2), F32),
            pltpu.VMEM((ng, 16, width // 2), BF16),
            pltpu.VMEM((ng, 16, width // 2), BF16),
            pltpu.VMEM((ng, 16, 256), F32),
            pltpu.VMEM((ng, 16, 256), F32),
            pltpu.VMEM((nm, 8, 256), F32),
            pltpu.VMEM((nm, 8, 256), F32),
            pltpu.VMEM((ng, nm * modes // ng, snaps), F32),
            pltpu.VMEM((ng, nm * modes // ng, snaps), F32),
            dma((4,)),
            dma((7, nchunk)),
            dma((nm, nchunk)),
            dma((4,)),
            dma((2, nm)),
            dma((2, nm)),
            dma((2, ng)),
            dma((2, ng)),
            dma((2, nm)),
            dma((2, ng)),
        ],
        compiler_params=pltpu.CompilerParams(
            collective_id=0, has_side_effects=True, vmem_limit_bytes=62 << 20
        ),
    )(state, basis, film_mask, sample_cells, owner.reshape(1, samp))


def solution(mesh):
    in_specs = (
        P(None, "mode", "grid", None),
        P("grid", None),
        P(None, "mode", "grid", None),
        P("grid", None),
        P("grid", None, None),
    )
    out_specs = (
        P("grid", "mode"),
        P(("grid", "mode"), None, None),
        P(("grid", "mode"), None),
        P(("grid", "mode"), None),
    )
    return jax.shard_map(
        functools.partial(per_device, mesh.shape["grid"], mesh.shape["mode"]),
        mesh=mesh, in_specs=in_specs, out_specs=out_specs, check_vma=False,
    )
```

```python
import functools

import jax
import jax.numpy as jnp
from jax import lax
from jax.experimental import pallas as pl
from jax.experimental.pallas import tpu as pltpu
from jax.sharding import PartitionSpec as P

MESH = pl.DeviceIdType.MESH
F32 = jnp.float32
BF16 = jnp.bfloat16


def dot_nt(a, b):
    return lax.dot_general(a, b, (((1,), (1,)), ((), ())), preferred_element_type=F32)


def kernel(
    ng, nm, weight,
    state, basis, mask, cell_row, own_row,
    o_red, o_samp, o_gram, o_proj,
    raw_b, raw_s, st, rate, gat, hot, slots,
    acc_p, picks, pbg, t1, t1r, relay, w32, w16, w16r, hb, hr, mb, mr, fb, fr,
    lsem, ssem, rsem, hsem, tsem, wsem, qsem, msem, fsem,
):
    g = lax.axis_index("grid")
    m = lax.axis_index("mode")
    ny = nm // 2
    c = lax.rem(m, 2)
    y = m // 2
    right = lax.rem(y + 1, ny) * 2 + c
    left = lax.rem(y + ny - 1, ny) * 2 + c
    opp = lax.rem(y + 2, ny) * 2 + c
    sib = y * 2 + (1 - c)
    flip = 1 - 2 * c
    modes = basis.shape[1]
    snaps = state.shape[1]
    nrow = state.shape[2]
    ncol = state.shape[3]
    samp = cell_row.shape[1]
    nchunk = 2 * nrow

    loads = []
    for s in range(2):
        loads.append(pltpu.make_async_copy(basis.at[s], raw_b.at[s], lsem.at[s]))
    for s in range(2):
        loads.append(pltpu.make_async_copy(state.at[s], raw_s.at[s], lsem.at[2 + s]))
    loads[0].start()
    loads[1].start()

    barrier = pltpu.get_barrier_semaphore()
    for d in range(1, nm):
        pl.semaphore_signal(barrier, inc=1, device_id=(g, lax.rem(m + d, nm)), device_id_type=MESH)
    for d in range(1, ng):
        pl.semaphore_signal(barrier, inc=1, device_id=(lax.rem(g + d, ng), m), device_id_type=MESH)
    pl.semaphore_wait(barrier, nm - 1 + ng - 1)

    sent = []

    def push(src, dst, send_sem, recv_sem, device):
        copy = pltpu.make_async_remote_copy(
            src_ref=src, dst_ref=dst, send_sem=send_sem, recv_sem=recv_sem,
            device_id=device, device_id_type=MESH,
        )
        copy.start()
        sent.append(copy)

    def await_recv(dst, send_sem, recv_sem):
        pltpu.make_async_remote_copy(
            src_ref=dst, dst_ref=dst, send_sem=send_sem, recv_sem=recv_sem,
            device_id=(g, sib), device_id_type=MESH,
        ).wait_recv()

    def slot(j, owner):
        return gat.at[j, owner] if j < nchunk else pbg.at[j - nchunk, owner]

    def ag_send(owner, j, kind, to):
        push(slot(j, owner), slot(j, owner), ssem.at[kind, j], rsem.at[owner, j], (g, to))

    def ag_recv(owner, j):
        await_recv(slot(j, owner), ssem.at[0, j], rsem.at[owner, j])

    def start(j):
        ag_send(m, j, 0, right)
        ag_send(m, j, 1, left)

    def near(j):
        ag_recv(left, j)
        ag_send(left, j, 4, sib)
        ag_recv(right, j)
        ag_send(right, j, 5, sib)

    def onward(j):
        if j % 2 == 0:
            ag_send(left, j, 3, right)
        else:
            ag_send(right, j, 3, left)

    def far(j):
        ag_recv(opp, j)
        ag_send(opp, j, 6, sib)

    def wait_sib(j):
        for owner in (sib, right + flip, left + flip, opp + flip):
            ag_recv(owner, j)

    def project(j):
        s, r = j // nrow, j % nrow
        wait_sib(j)
        block = gat[j].reshape(nm * modes, ncol)
        part = dot_nt(block, rate[r, s * snaps : (s + 1) * snaps, :])
        fb[...] += part.reshape(fb.shape)

    for s in range(2):
        loads[s].wait()
        if s == 0:
            loads[2].start()
            loads[3].start()
        mine = jnp.swapaxes(raw_b[s], 0, 1)
        gat[pl.ds(s * nrow, nrow), m] = mine
        for j in range(s * nrow, (s + 1) * nrow):
            if j < nchunk - 2:
                start(j)
        rate[:, 2 * snaps + s * modes : 2 * snaps + (s + 1) * modes] = mine
    for j in range(nchunk):
        ag_send(m, j, 2, sib)

    step = 16
    loads[2].wait()

    def split_s(i, carry):
        rows = pl.ds(pl.multiple_of(i * step, step), step)
        st[pl.ds(1, nrow), rows] = jnp.swapaxes(raw_s[0, rows], 0, 1)
        return carry

    lax.fori_loop(0, snaps // step, split_s, 0)
    up_dev = lax.rem(g + 1, ng)
    down_dev = lax.rem(g + ng - 1, ng)
    push(st.at[nrow], st.at[0], hsem.at[0], hsem.at[1], (up_dev, m))
    push(st.at[1], st.at[nrow + 1], hsem.at[2], hsem.at[3], (down_dev, m))
    loads[3].wait()

    def split_b(i, carry):
        rows = pl.ds(pl.multiple_of(i * step, step), step)
        high = pl.ds(pl.multiple_of(i * step + snaps, step), step)
        rate[:, high] = jnp.swapaxes(raw_s[1, rows], 0, 1)
        return carry

    lax.fori_loop(0, snaps // step, split_b, 0)

    lane = lax.broadcasted_iota(jnp.int32, (step, ncol), 1)

    def rates(r):
        film = jnp.broadcast_to(mask[pl.ds(r, 1), :].astype(F32), (step, ncol))
        up_on = jnp.where(jnp.logical_and(r == 0, g == 0), 0.0, 1.0).astype(F32)
        down_on = jnp.where(jnp.logical_and(r == nrow - 1, g == ng - 1), 0.0, 1.0).astype(F32)

        def body(i, carry):
            rows = pl.ds(pl.multiple_of(i * step, step), step)
            high = pl.ds(pl.multiple_of(i * step + snaps, step), step)
            sub = st[r + 1, rows].astype(F32)
            up = st[r, rows].astype(F32) * up_on
            down = st[r + 2, rows].astype(F32) * down_on
            bio = rate[r, high].astype(F32)
            before = jnp.where(lane == 0, 0.0, pltpu.roll(sub, 1, 1))
            after = jnp.where(lane == ncol - 1, 0.0, pltpu.roll(sub, ncol - 1, 1))
            lap = down + up + after + before - 4.0 * sub
            taken = bio * (sub / (0.5 + sub))
            rate[r, rows] = ((1.0 - 0.2 * film) * lap - 2.0 * taken).astype(BF16)
            rate[r, high] = (film * (taken - 0.1 * bio)).astype(BF16)
            return carry

        lax.fori_loop(0, snaps // step, body, 0)

    cells = cell_row[...].astype(F32)
    part_rows = 512

    def pick(r):
        def build(i, carry):
            base = (r * ncol + i * part_rows).astype(F32)
            number = lax.broadcasted_iota(jnp.int32, (part_rows, samp), 0).astype(F32) + base
            rows = pl.ds(pl.multiple_of(i * part_rows, part_rows), part_rows)
            hot[rows] = jnp.where(number == cells, 1.0, 0.0).astype(BF16)
            return carry

        lax.fori_loop(0, ncol // part_rows, build, 0)
        acc_p[...] += jnp.dot(rate[r], hot[...], preferred_element_type=F32)

    acc_p[...] = jnp.zeros(acc_p.shape, F32)
    fb[...] = jnp.zeros(fb.shape, F32)
    rates(1)
    near(0)
    rates(2)
    pick(1)
    near(1)
    pick(2)
    near(2)

    ii = lax.broadcasted_iota(jnp.int32, (samp, samp), 0)
    jj = lax.broadcasted_iota(jnp.int32, (samp, samp), 1)
    own = jnp.broadcast_to(own_row[...].astype(F32), (samp, samp))
    own_col = jnp.sum(jnp.where(ii == jj, own, 0.0), axis=1, keepdims=True)
    same = jnp.logical_and(own == own_col, ii < jj)
    rank = jnp.sum(jnp.where(same, 1.0, 0.0), axis=0, keepdims=True)
    own_f = own_row[...].astype(F32)
    own_hi = jnp.floor(own_f * (1.0 / nm))
    key = (own_f - own_hi * nm) * 128.0 + own_hi * 8.0 + rank
    for mm in range(nm):
        number = lax.broadcasted_iota(jnp.int32, (128, samp), 0).astype(F32) + float(mm * 128)
        slots[mm] = jnp.where(number == key, 1.0, 0.0).astype(BF16)

    near(3)
    onward(0)
    onward(1)
    await_recv(st.at[0], hsem.at[0], hsem.at[1])
    await_recv(st.at[nrow + 1], hsem.at[2], hsem.at[3])
    rates(0)
    near(4)
    pick(0)
    rates(nrow - 1)
    pick(nrow - 1)
    picks[...] = acc_p[...].astype(BF16)
    for s in range(2):
        pbg[s, m] = picks[2 * snaps + s * modes : 2 * snaps + (s + 1) * modes, :]
    for mm in range(nm):
        t1[mm] = dot_nt(slots[mm], picks[0 : 2 * snaps, :]).astype(BF16)

    def row_send(src, dst, n, origin, to):
        push(src, dst, tsem.at[0, n], tsem.at[1, origin], (g, to))

    def row_recv(dst, origin):
        await_recv(dst, tsem.at[0, 0], tsem.at[1, origin])

    for j in range(nchunk, nchunk + 2):
        start(j)
    row_send(t1.at[opp], relay.at[0], 0, nm, right)
    row_send(t1.at[opp + flip], relay.at[1], 1, nm + 1, left)
    row_send(t1.at[right], t1r.at[m], 2, m, right)
    row_send(t1.at[left], t1r.at[m], 3, m, left)
    row_send(t1.at[right + flip], t1r.at[m], 4, m, right + flip)
    row_send(t1.at[left + flip], t1r.at[m], 5, m, left + flip)
    start(nchunk - 2)
    row_send(t1.at[sib], t1r.at[m], 6, m, sib)
    for j in range(nchunk, nchunk + 2):
        ag_send(m, j, 2, sib)
    t1r[m] = t1[m]
    near(5)
    far(0)
    far(1)
    project(0)
    project(1)
    for j in range(nchunk, nchunk + 2):
        near(j)
        onward(j)
    row_recv(relay.at[0], nm)
    row_send(relay.at[0], t1r.at[left], 7, left, right)
    row_recv(relay.at[1], nm + 1)
    row_send(relay.at[1], t1r.at[right], 8, right, left + flip)
    start(nchunk - 1)
    for j in range(2, 6):
        onward(j)
    near(6)
    onward(6)
    for j in range(nchunk, nchunk + 2):
        far(j)
    for j in range(nchunk, nchunk + 2):
        wait_sib(j)

    hyper = jnp.zeros((nm * modes, snaps), F32)
    gram = jnp.zeros((nm * modes, modes), F32)
    for s in range(2):
        all_modes = pbg[s].reshape(nm * modes, samp)
        hyper = hyper + dot_nt(all_modes, picks[s * snaps : (s + 1) * snaps, :])
        gram = gram + dot_nt(all_modes, pbg[s, m])
        w32[:, 0:8, s * 256 : (s + 1) * 256] = dot_nt(slots[m], all_modes).reshape(ng, 8, nm * modes)
    hb[...] = jnp.zeros(hb.shape, F32)
    hb[:, :, 0:128] = (weight * hyper).reshape(ng, 16, snaps)
    hb[:, :, 128 : 128 + modes] = (weight * gram).reshape(ng, 16, modes)
    for d in range(1, ng):
        to = lax.rem(g + d, ng)
        push(hb.at[to], hr.at[g], qsem.at[0, d], qsem.at[1, d], (to, m))
    hr[g] = hb[g]

    for frm in (sib, right, right + flip, left, left + flip, opp, opp + flip):
        row_recv(t1r.at[frm], frm)
    half = w32.shape[2]
    for mm in range(nm):
        for s in range(2):
            col = 2 * nm * modes + s * nm * snaps + mm * snaps
            block = t1r[mm, :, s * snaps : (s + 1) * snaps].astype(F32).reshape(ng, 8, snaps)
            if col < half:
                w32[:, 0:8, col : col + snaps] = block
            else:
                w32[:, 8:16, col - half : col - half + snaps] = block
    w16[...] = w32[...].astype(BF16)
    for d in range(1, ng):
        to = lax.rem(g + d, ng)
        push(w16.at[to], w16r.at[g], wsem.at[0, d], wsem.at[1, d], (to, m))
    w16r[g] = w16[g]

    near(7)
    onward(7)
    for d in range(1, ng):
        frm = lax.rem(g + ng - d, ng)
        await_recv(hr.at[frm], qsem.at[0, d], qsem.at[1, d])
    total = jnp.sum(hr[...], axis=0)
    mb[...] = jnp.zeros(mb.shape, F32)
    for mm in range(nm):
        mb[mm, 0:2, :] = total[2 * mm : 2 * mm + 2, :]
    for d in range(1, nm):
        to = lax.rem(m + d, nm)
        push(mb.at[to], mr.at[m], msem.at[0, d], msem.at[1, d], (g, to))
    mr[m] = mb[m]
    far(2)
    far(3)
    project(2)
    project(3)
    for d in range(1, ng):
        frm = lax.rem(g + ng - d, ng)
        await_recv(w16r.at[frm], wsem.at[0, d], wsem.at[1, d])
    for h in range(2):
        part = w16r[...].astype(F32)[:, 8 * h : 8 * h + 8, :].reshape(ng * 8, half)
        o_samp[0, :, h * half : (h + 1) * half] = part.astype(BF16)
    for d in range(1, nm):
        frm = lax.rem(m + nm - d, nm)
        await_recv(mr.at[frm], msem.at[0, d], msem.at[1, d])
    for mm in range(nm):
        o_proj[:, mm * snaps : (mm + 1) * snaps] = mr[mm, 0:2, 0:snaps]
        o_gram[:, mm * modes : (mm + 1) * modes] = mr[mm, 0:2, 128 : 128 + modes]
    far(4)
    far(5)
    project(4)
    project(5)
    far(6)
    far(7)
    project(6)
    project(7)

    for d in range(1, ng):
        to = lax.rem(g + d, ng)
        push(fb.at[to], fr.at[g], fsem.at[0, d], fsem.at[1, d], (to, m))
    fr[g] = fb[g]
    for d in range(1, ng):
        frm = lax.rem(g + ng - d, ng)
        await_recv(fr.at[frm], fsem.at[0, d], fsem.at[1, d])
    o_red[...] = jnp.sum(fr[...], axis=0)
    for copy in sent:
        copy.wait_send()


def finish(*refs):
    for source, target in zip(refs[:4], refs[4:]):
        target[...] = source[...]


def per_device(ng, nm, state, film_mask, basis, sample_cells, owner):
    modes, snaps = basis.shape[1], state.shape[1]
    nrow, ncol = state.shape[2:]
    samp = sample_cells.shape[1]
    nchunk = 2 * nrow
    width = 2 * nm * (modes + snaps)
    dma = pltpu.SemaphoreType.DMA
    vmem = pl.BlockSpec(memory_space=pltpu.VMEM)
    hbm = pl.BlockSpec(memory_space=pl.ANY)
    outs = pl.pallas_call(
        functools.partial(kernel, ng, nm, nrow * ncol / samp),
        out_shape=(
            jax.ShapeDtypeStruct((nm * modes // ng, snaps), F32),
            jax.ShapeDtypeStruct((1, ng * 8, width), BF16),
            jax.ShapeDtypeStruct((2, nm * modes), F32),
            jax.ShapeDtypeStruct((2, nm * snaps), F32),
        ),
        in_specs=[hbm, hbm, vmem, vmem, vmem],
        out_specs=(vmem, vmem, vmem, vmem),
        scratch_shapes=[
            pltpu.VMEM((2, modes, nrow, ncol), BF16),
            pltpu.VMEM((2, snaps, nrow, ncol), BF16),
            pltpu.VMEM((nrow + 2, snaps, ncol), BF16),
            pltpu.VMEM((nrow, 2 * (snaps + modes), ncol), BF16),
            pltpu.VMEM((nchunk, nm, modes, ncol), BF16),
            pltpu.VMEM((ncol, samp), BF16),
            pltpu.VMEM((nm, 128, samp), BF16),
            pltpu.VMEM((2 * (snaps + modes), samp), F32),
            pltpu.VMEM((2 * (snaps + modes), samp), BF16),
            pltpu.VMEM((2, nm, modes, samp), BF16),
            pltpu.VMEM((nm, 128, 2 * snaps), BF16),
            pltpu.VMEM((nm, 128, 2 * snaps), BF16),
            pltpu.VMEM((2, 128, 2 * snaps), BF16),
            pltpu.VMEM((ng, 16, width // 2), F32),
            pltpu.VMEM((ng, 16, width // 2), BF16),
            pltpu.VMEM((ng, 16, width // 2), BF16),
            pltpu.VMEM((ng, 16, 256), F32),
            pltpu.VMEM((ng, 16, 256), F32),
            pltpu.VMEM((nm, 8, 256), F32),
            pltpu.VMEM((nm, 8, 256), F32),
            pltpu.VMEM((ng, nm * modes // ng, snaps), F32),
            pltpu.VMEM((ng, nm * modes // ng, snaps), F32),
            dma((4,)),
            dma((7, nchunk + 2)),
            dma((nm, nchunk + 2)),
            dma((4,)),
            dma((2, nm + 2)),
            dma((2, ng)),
            dma((2, ng)),
            dma((2, nm)),
            dma((2, ng)),
        ],
        compiler_params=pltpu.CompilerParams(
            collective_id=0, has_side_effects=True, vmem_limit_bytes=62 << 20
        ),
    )(state, basis, film_mask, sample_cells, owner.reshape(1, samp))
    return pl.pallas_call(
        finish,
        out_shape=tuple(jax.ShapeDtypeStruct(o.shape, o.dtype) for o in outs),
        in_specs=[vmem] * 4,
        out_specs=(vmem,) * 4,
    )(*outs)


def solution(mesh):
    in_specs = (
        P(None, "mode", "grid", None),
        P("grid", None),
        P(None, "mode", "grid", None),
        P("grid", None),
        P("grid", None, None),
    )
    out_specs = (
        P("grid", "mode"),
        P(("grid", "mode"), None, None),
        P(("grid", "mode"), None),
        P(("grid", "mode"), None),
    )
    return jax.shard_map(
        functools.partial(per_device, mesh.shape["grid"], mesh.shape["mode"]),
        mesh=mesh, in_specs=in_specs, out_specs=out_specs, check_vma=False,
    )
```

```python
import functools

import jax
import jax.numpy as jnp
from jax import lax
from jax.experimental import pallas as pl
from jax.experimental.pallas import tpu as pltpu
from jax.sharding import PartitionSpec as P

MESH = pl.DeviceIdType.MESH
F32 = jnp.float32
BF16 = jnp.bfloat16


def dot_nt(a, b):
    return lax.dot_general(a, b, (((1,), (1,)), ((), ())), preferred_element_type=F32)


def kernel(
    ng, nm, weight,
    state, basis, mask, cell_row, own_row,
    o_red, o_samp, o_gram, o_proj,
    raw_b, raw_s, st, rate, gat, hot, slots,
    acc_p, picks, pbg, t0, t0r, t1, t1r, relay, w32, w16, w16r, hb, hr, mb, mr, acc_n, acc_f, fb, fr,
    lsem, ssem, rsem, hsem, tsem, gsem, wsem, qsem, msem, fsem,
):
    g = lax.axis_index("grid")
    m = lax.axis_index("mode")
    ny = nm // 2
    c = lax.rem(m, 2)
    y = m // 2
    right = lax.rem(y + 1, ny) * 2 + c
    left = lax.rem(y + ny - 1, ny) * 2 + c
    opp = lax.rem(y + 2, ny) * 2 + c
    sib = y * 2 + (1 - c)
    flip = 1 - 2 * c
    modes = basis.shape[1]
    snaps = state.shape[1]
    nrow = state.shape[2]
    ncol = state.shape[3]
    samp = cell_row.shape[1]
    nchunk = 2 * nrow

    half_col = ncol // 2
    loads = [
        pltpu.make_async_copy(basis.at[0, :, :, 0:half_col], raw_b.at[0, :, :, 0:half_col], lsem.at[0]),
        pltpu.make_async_copy(basis.at[0, :, :, half_col:ncol], raw_b.at[0, :, :, half_col:ncol], lsem.at[1]),
        pltpu.make_async_copy(basis.at[1], raw_b.at[1], lsem.at[2]),
        pltpu.make_async_copy(state.at[0], raw_s.at[0], lsem.at[3]),
        pltpu.make_async_copy(state.at[1], raw_s.at[1], lsem.at[4]),
    ]
    for load in loads[:3]:
        load.start()

    barrier = pltpu.get_barrier_semaphore()
    for d in range(1, nm):
        pl.semaphore_signal(barrier, inc=1, device_id=(g, lax.rem(m + d, nm)), device_id_type=MESH)
    for d in range(1, ng):
        pl.semaphore_signal(barrier, inc=1, device_id=(lax.rem(g + d, ng), m), device_id_type=MESH)

    sent = []

    def push(src, dst, send_sem, recv_sem, device):
        copy = pltpu.make_async_remote_copy(
            src_ref=src, dst_ref=dst, send_sem=send_sem, recv_sem=recv_sem,
            device_id=device, device_id_type=MESH,
        )
        copy.start()
        sent.append(copy)

    def await_recv(dst, send_sem, recv_sem):
        pltpu.make_async_remote_copy(
            src_ref=dst, dst_ref=dst, send_sem=send_sem, recv_sem=recv_sem,
            device_id=(g, sib), device_id_type=MESH,
        ).wait_recv()

    pieces = [(k, 2, col, half_col) for col in (0, half_col) for k in (0, 2)]
    pieces += [(k, 1, 0, ncol) for k in (4, 5)]
    pieces += [(k, 1, col, half_col) for col in (0, half_col) for k in (6, 7)]
    npiece = len(pieces)
    seen = (m, right, left, opp)

    def slot(j, rel, owner):
        if j < npiece:
            k, count, col, size = pieces[j]
            return gat.at[k : k + count, rel, c, :, col : col + size]
        return pbg.at[j - npiece, owner]

    def slot_sib(j, rel):
        if j < npiece:
            k, count, col, size = pieces[j]
            return gat.at[k : k + count, rel, 1 - c, :, col : col + size]
        return pbg.at[j - npiece, seen[rel] + flip]

    def ag_send(j, rel, there, kind, to):
        push(
            slot(j, rel, seen[rel]), slot(j, there, seen[rel]),
            ssem.at[kind, j], rsem.at[there, c, j], (g, to),
        )

    def ag_recv(j, rel):
        await_recv(slot(j, rel, seen[rel]), ssem.at[0, j], rsem.at[rel, c, j])

    def start(j):
        ag_send(j, 0, 2, 0, right)
        ag_send(j, 0, 1, 1, left)

    def near(j):
        ag_recv(j, 2)
        ag_send(j, 2, 2, 4, sib)
        ag_recv(j, 1)
        ag_send(j, 1, 1, 5, sib)

    def onward(j):
        if j % 2 == 0:
            ag_send(j, 2, 3, 3, right)
        else:
            ag_send(j, 1, 3, 3, left)

    def far(j):
        ag_recv(j, 3)
        ag_send(j, 3, 3, 6, sib)

    def wait_sib(j, rels):
        for rel in rels:
            await_recv(slot_sib(j, rel), ssem.at[0, j], rsem.at[rel, 1 - c, j])

    def project(j, acc, low, high):
        first, count, col, size = pieces[j]
        wait_sib(j, range(low, high))
        for k in range(first, first + count):
            s, r = k // nrow, k % nrow
            block = gat[k, low:high, :, :, col : col + size].reshape(acc.shape[0], size)
            acc[...] += dot_nt(block, rate[r, s * snaps : (s + 1) * snaps, col : col + size])

    def project_near(j):
        project(j, acc_n, 0, 3)

    def project_far(j):
        project(j, acc_f, 3, 4)

    def split_basis(s, col, size):
        mine = jnp.swapaxes(raw_b[s, :, :, col : col + size], 0, 1)
        gat[pl.ds(s * nrow, nrow), 0, c, :, col : col + size] = mine
        rate[:, 2 * snaps + s * modes : 2 * snaps + (s + 1) * modes, col : col + size] = mine

    loads[0].wait()
    split_basis(0, 0, half_col)
    pl.semaphore_wait(barrier, nm - 1 + ng - 1)
    start(0)
    start(1)
    loads[1].wait()
    split_basis(0, half_col, half_col)
    start(2)
    start(3)
    loads[2].wait()
    loads[3].start()
    loads[4].start()
    split_basis(1, 0, ncol)
    start(4)
    start(5)
    for j in range(npiece):
        ag_send(j, 0, 0, 2, sib)

    step = 16
    loads[3].wait()

    def split_s(i, carry):
        rows = pl.ds(pl.multiple_of(i * step, step), step)
        st[pl.ds(1, nrow), rows] = jnp.swapaxes(raw_s[0, rows], 0, 1)
        return carry

    lax.fori_loop(0, snaps // step, split_s, 0)
    up_dev = lax.rem(g + 1, ng)
    down_dev = lax.rem(g + ng - 1, ng)
    push(st.at[nrow], st.at[0], hsem.at[0], hsem.at[1], (up_dev, m))
    push(st.at[1], st.at[nrow + 1], hsem.at[2], hsem.at[3], (down_dev, m))
    loads[4].wait()

    def split_b(i, carry):
        rows = pl.ds(pl.multiple_of(i * step, step), step)
        high = pl.ds(pl.multiple_of(i * step + snaps, step), step)
        rate[:, high] = jnp.swapaxes(raw_s[1, rows], 0, 1)
        return carry

    lax.fori_loop(0, snaps // step, split_b, 0)

    lane = lax.broadcasted_iota(jnp.int32, (step, ncol), 1)

    def rates(r):
        film = jnp.broadcast_to(mask[pl.ds(r, 1), :].astype(F32), (step, ncol))
        up_on = jnp.where(jnp.logical_and(r == 0, g == 0), 0.0, 1.0).astype(F32)
        down_on = jnp.where(jnp.logical_and(r == nrow - 1, g == ng - 1), 0.0, 1.0).astype(F32)

        def body(i, carry):
            rows = pl.ds(pl.multiple_of(i * step, step), step)
            high = pl.ds(pl.multiple_of(i * step + snaps, step), step)
            sub = st[r + 1, rows].astype(F32)
            up = st[r, rows].astype(F32) * up_on
            down = st[r + 2, rows].astype(F32) * down_on
            bio = rate[r, high].astype(F32)
            before = jnp.where(lane == 0, 0.0, pltpu.roll(sub, 1, 1))
            after = jnp.where(lane == ncol - 1, 0.0, pltpu.roll(sub, ncol - 1, 1))
            lap = down + up + after + before - 4.0 * sub
            taken = bio * (sub / (0.5 + sub))
            rate[r, rows] = ((1.0 - 0.2 * film) * lap - 2.0 * taken).astype(BF16)
            rate[r, high] = (film * (taken - 0.1 * bio)).astype(BF16)
            return carry

        lax.fori_loop(0, snaps // step, body, 0)

    cells = cell_row[...].astype(F32)
    part_rows = 512

    def pick(r):
        def build(i, carry):
            base = (r * ncol + i * part_rows).astype(F32)
            number = lax.broadcasted_iota(jnp.int32, (part_rows, samp), 0).astype(F32) + base
            rows = pl.ds(pl.multiple_of(i * part_rows, part_rows), part_rows)
            hot[rows] = jnp.where(number == cells, 1.0, 0.0).astype(BF16)
            return carry

        lax.fori_loop(0, ncol // part_rows, build, 0)
        acc_p[...] += jnp.dot(rate[r], hot[...], preferred_element_type=F32)

    acc_p[...] = jnp.zeros(acc_p.shape, F32)
    acc_n[...] = jnp.zeros(acc_n.shape, F32)
    acc_f[...] = jnp.zeros(acc_f.shape, F32)
    rates(1)
    near(0)
    rates(2)
    pick(1)
    near(1)
    pick(2)
    near(2)

    ii = lax.broadcasted_iota(jnp.int32, (samp, samp), 0)
    jj = lax.broadcasted_iota(jnp.int32, (samp, samp), 1)
    own = jnp.broadcast_to(own_row[...].astype(F32), (samp, samp))
    own_col = jnp.sum(jnp.where(ii == jj, own, 0.0), axis=1, keepdims=True)
    same = jnp.logical_and(own == own_col, ii < jj)
    rank = jnp.sum(jnp.where(same, 1.0, 0.0), axis=0, keepdims=True)
    own_f = own_row[...].astype(F32)
    own_hi = jnp.floor(own_f * (1.0 / nm))
    own_lo = own_f - own_hi * nm
    key = own_f * 8.0 + rank
    for gg in range(ng):
        number = lax.broadcasted_iota(jnp.int32, (8 * nm, samp), 0).astype(F32) + float(gg * 8 * nm)
        slots[gg] = jnp.where(number == key, 1.0, 0.0).astype(BF16)
    key = jnp.where(own_lo == m.astype(F32), own_hi * 8.0 + rank, -1.0)
    number = lax.broadcasted_iota(jnp.int32, (8 * ng, samp), 0).astype(F32)
    mine = jnp.where(number == key, 1.0, 0.0).astype(BF16)

    near(3)
    onward(0)
    onward(1)
    await_recv(st.at[0], hsem.at[0], hsem.at[1])
    await_recv(st.at[nrow + 1], hsem.at[2], hsem.at[3])
    rates(0)
    near(4)
    pick(0)
    rates(nrow - 1)
    pick(nrow - 1)
    picks[...] = acc_p[...].astype(BF16)
    for s in range(2):
        pbg[s, m] = picks[2 * snaps + s * modes : 2 * snaps + (s + 1) * modes, :]
    picked = (npiece, npiece + 1)
    for j in picked:
        start(j)
    start(6)
    start(7)
    for j in picked:
        ag_send(j, 0, 0, 2, sib)
    rows = dot_nt(slots[...].reshape(8 * nm * ng, samp), picks[0 : 2 * snaps, :])
    t0[...] = rows.astype(BF16).reshape(t0.shape)
    for d in range(1, ng):
        to = lax.rem(g + d, ng)
        push(t0.at[to], t0r.at[g], gsem.at[0, d], gsem.at[1, d], (to, m))
    t0r[g] = t0[g]

    def row_send(src, dst, n, origin, to):
        push(src, dst, tsem.at[0, n], tsem.at[1, origin], (g, to))

    def row_recv(dst, origin):
        await_recv(dst, tsem.at[0, 0], tsem.at[1, origin])

    near(5)
    for j in range(6):
        project_near(j)
    far(0)
    far(1)
    for j in picked:
        near(j)
        onward(j)
    start(8)
    start(9)
    for j in range(2, 6):
        onward(j)
    project_far(0)
    project_far(1)
    near(6)
    onward(6)
    near(7)
    onward(7)
    for j in picked:
        far(j)
    for j in picked:
        wait_sib(j, range(4))

    hyper = jnp.zeros((nm * modes, snaps), F32)
    gram = jnp.zeros((nm * modes, modes), F32)
    for s in range(2):
        all_modes = pbg[s].reshape(nm * modes, samp)
        hyper = hyper + dot_nt(all_modes, picks[s * snaps : (s + 1) * snaps, :])
        gram = gram + dot_nt(all_modes, pbg[s, m])
        w32[:, 8 * s : 8 * s + 8, :] = dot_nt(mine, all_modes).reshape(ng, 8, nm * modes)
    hb[...] = jnp.zeros(hb.shape, F32)
    hb[:, :, 0:128] = (weight * hyper).reshape(ng, 16, snaps)
    hb[:, :, 128 : 128 + modes] = (weight * gram).reshape(ng, 16, modes)
    for d in range(1, ng):
        to = lax.rem(g + d, ng)
        push(hb.at[to], hr.at[g], qsem.at[0, d], qsem.at[1, d], (to, m))
    hr[g] = hb[g]

    w16[...] = w32[...].astype(BF16)
    for d in range(1, ng):
        to = lax.rem(g + d, ng)
        push(w16.at[to], w16r.at[g], wsem.at[0, d], wsem.at[1, d], (to, m))
    w16r[g] = w16[g]

    for d in range(1, ng):
        frm = lax.rem(g + ng - d, ng)
        await_recv(t0r.at[frm], gsem.at[0, d], gsem.at[1, d])
    for mm in range(nm):
        t1[mm] = t0r[...].astype(F32)[:, 8 * mm : 8 * mm + 8, :].reshape(ng * 8, 2 * snaps).astype(BF16)
    near(8)
    onward(8)
    near(9)
    onward(9)
    settled = len(sent) - 6
    for d in range(1, ng):
        frm = lax.rem(g + ng - d, ng)
        await_recv(hr.at[frm], qsem.at[0, d], qsem.at[1, d])
    total = jnp.sum(hr[...], axis=0)
    mb[...] = jnp.zeros(mb.shape, F32)
    for mm in range(nm):
        mb[mm, 0:2, :] = total[2 * mm : 2 * mm + 2, :]
    for d in range(1, nm):
        to = lax.rem(m + d, nm)
        push(mb.at[to], mr.at[m], msem.at[0, d], msem.at[1, d], (g, to))
    mr[m] = mb[m]
    row_send(t1.at[opp], relay.at[0], 0, nm, right)
    row_send(t1.at[opp + flip], relay.at[1], 1, nm + 1, left)
    row_send(t1.at[right], t1r.at[m], 2, m, right)
    row_send(t1.at[left], t1r.at[m], 3, m, left)
    row_send(t1.at[right + flip], t1r.at[m], 4, m, right + flip)
    row_send(t1.at[left + flip], t1r.at[m], 5, m, left + flip)
    row_send(t1.at[sib], t1r.at[m], 6, m, sib)
    t1r[m] = t1[m]
    for j in range(6, 10):
        project_near(j)

    per_chip = ng // ny
    opp_chip = lax.rem(y + 2, ny)
    for rel in range(3):
        fb[pl.ds(per_chip * (seen[rel] // 2), per_chip)] = acc_n[
            rel * 2 * modes : (rel + 1) * 2 * modes
        ].reshape(per_chip, fb.shape[1], snaps)

    def sums(late):
        for d in range(1, ng):
            to = lax.rem(g + d, ng)
            copy = pltpu.make_async_remote_copy(
                src_ref=fb.at[to], dst_ref=fr.at[g], send_sem=fsem.at[0, d], recv_sem=fsem.at[1, d],
                device_id=(to, m), device_id_type=MESH,
            )
            pl.when((to // per_chip == opp_chip) == late)(copy.start)
            if late:
                sent.append(copy)

    sums(False)
    far(2)
    far(3)
    project_far(2)
    project_far(3)
    for d in range(1, ng):
        frm = lax.rem(g + ng - d, ng)
        await_recv(w16r.at[frm], wsem.at[0, d], wsem.at[1, d])
    for s in range(2):
        part = w16r[...].astype(F32)[:, 8 * s : 8 * s + 8, :].reshape(ng * 8, nm * modes)
        o_samp[0, :, s * nm * modes : (s + 1) * nm * modes] = part.astype(BF16)
    far(4)
    far(5)
    project_far(4)
    project_far(5)
    for copy in sent[:settled]:
        copy.wait_send()
    del sent[:settled]
    far(6)
    far(7)
    project_far(6)
    project_far(7)
    far(8)
    far(9)
    row_recv(relay.at[0], nm)
    row_send(relay.at[0], t1r.at[left], 7, left, right)
    row_recv(relay.at[1], nm + 1)
    row_send(relay.at[1], t1r.at[right], 8, right, left + flip)
    project_far(8)
    project_far(9)
    fb[pl.ds(per_chip * opp_chip, per_chip)] = acc_f[...].reshape(per_chip, fb.shape[1], snaps)
    sums(True)
    fr[g] = fb[g]
    for frm in (sib, right, right + flip, left, left + flip, opp, opp + flip):
        row_recv(t1r.at[frm], frm)
    for mm in range(nm):
        for s in range(2):
            col = 2 * nm * modes + s * nm * snaps + mm * snaps
            o_samp[0, :, col : col + snaps] = t1r[mm, :, s * snaps : (s + 1) * snaps]
    for d in range(1, nm):
        frm = lax.rem(m + nm - d, nm)
        await_recv(mr.at[frm], msem.at[0, d], msem.at[1, d])
    for mm in range(nm):
        o_proj[:, mm * snaps : (mm + 1) * snaps] = mr[mm, 0:2, 0:snaps]
        o_gram[:, mm * modes : (mm + 1) * modes] = mr[mm, 0:2, 128 : 128 + modes]
    for d in range(1, ng):
        frm = lax.rem(g + ng - d, ng)
        await_recv(fr.at[frm], fsem.at[0, d], fsem.at[1, d])
    o_red[...] = jnp.sum(fr[...], axis=0)
    for copy in sent:
        copy.wait_send()


def finish(*refs):
    for source, target in zip(refs[:4], refs[4:]):
        target[...] = source[...]


def per_device(ng, nm, state, film_mask, basis, sample_cells, owner):
    modes, snaps = basis.shape[1], state.shape[1]
    nrow, ncol = state.shape[2:]
    samp = sample_cells.shape[1]
    nchunk = 2 * nrow
    width = 2 * nm * (modes + snaps)
    dma = pltpu.SemaphoreType.DMA
    vmem = pl.BlockSpec(memory_space=pltpu.VMEM)
    hbm = pl.BlockSpec(memory_space=pl.ANY)
    outs = pl.pallas_call(
        functools.partial(kernel, ng, nm, nrow * ncol / samp),
        out_shape=(
            jax.ShapeDtypeStruct((nm * modes // ng, snaps), F32),
            jax.ShapeDtypeStruct((1, ng * 8, width), BF16),
            jax.ShapeDtypeStruct((2, nm * modes), F32),
            jax.ShapeDtypeStruct((2, nm * snaps), F32),
        ),
        in_specs=[hbm, hbm, vmem, vmem, vmem],
        out_specs=(vmem, vmem, vmem, vmem),
        scratch_shapes=[
            pltpu.VMEM((2, modes, nrow, ncol), BF16),
            pltpu.VMEM((2, snaps, nrow, ncol), BF16),
            pltpu.VMEM((nrow + 2, snaps, ncol), BF16),
            pltpu.VMEM((nrow, 2 * (snaps + modes), ncol), BF16),
            pltpu.VMEM((nchunk, nm // 2, 2, modes, ncol), BF16),
            pltpu.VMEM((ncol, samp), BF16),
            pltpu.VMEM((ng, 8 * nm, samp), BF16),
            pltpu.VMEM((2 * (snaps + modes), samp), F32),
            pltpu.VMEM((2 * (snaps + modes), samp), BF16),
            pltpu.VMEM((2, nm, modes, samp), BF16),
            pltpu.VMEM((ng, 8 * nm, 2 * snaps), BF16),
            pltpu.VMEM((ng, 8 * nm, 2 * snaps), BF16),
            pltpu.VMEM((nm, 8 * ng, 2 * snaps), BF16),
            pltpu.VMEM((nm, 8 * ng, 2 * snaps), BF16),
            pltpu.VMEM((2, 128, 2 * snaps), BF16),
            pltpu.VMEM((ng, 16, nm * modes), F32),
            pltpu.VMEM((ng, 16, nm * modes), BF16),
            pltpu.VMEM((ng, 16, nm * modes), BF16),
            pltpu.VMEM((ng, 16, 256), F32),
            pltpu.VMEM((ng, 16, 256), F32),
            pltpu.VMEM((nm, 8, 256), F32),
            pltpu.VMEM((nm, 8, 256), F32),
            pltpu.VMEM((6 * modes, snaps), F32),
            pltpu.VMEM((2 * modes, snaps), F32),
            pltpu.VMEM((ng, nm * modes // ng, snaps), F32),
            pltpu.VMEM((ng, nm * modes // ng, snaps), F32),
            dma((5,)),
            dma((7, nchunk + 4)),
            dma((4, 2, nchunk + 4)),
            dma((4,)),
            dma((2, nm + 2)),
            dma((2, ng)),
            dma((2, ng)),
            dma((2, ng)),
            dma((2, nm)),
            dma((2, ng)),
        ],
        compiler_params=pltpu.CompilerParams(
            collective_id=0, has_side_effects=True, vmem_limit_bytes=56 << 20
        ),
    )(state, basis, film_mask, sample_cells, owner.reshape(1, samp))
    return pl.pallas_call(
        finish,
        out_shape=tuple(jax.ShapeDtypeStruct(o.shape, o.dtype) for o in outs),
        in_specs=[vmem] * 4,
        out_specs=(vmem,) * 4,
    )(*outs)


def solution(mesh):
    in_specs = (
        P(None, "mode", "grid", None),
        P("grid", None),
        P(None, "mode", "grid", None),
        P("grid", None),
        P("grid", None, None),
    )
    out_specs = (
        P("grid", "mode"),
        P(("grid", "mode"), None, None),
        P(("grid", "mode"), None),
        P(("grid", "mode"), None),
    )
    return jax.shard_map(
        functools.partial(per_device, mesh.shape["grid"], mesh.shape["mode"]),
        mesh=mesh, in_specs=in_specs, out_specs=out_specs, check_vma=False,
    )
```

```python
import functools

import jax
import jax.numpy as jnp
from jax import lax
from jax.experimental import pallas as pl
from jax.experimental.pallas import tpu as pltpu
from jax.sharding import PartitionSpec as P

MESH = pl.DeviceIdType.MESH
F32 = jnp.float32
BF16 = jnp.bfloat16


def dot_nt(a, b):
    return lax.dot_general(a, b, (((1,), (1,)), ((), ())), preferred_element_type=F32)


def kernel(
    ng, nm, weight,
    state, basis, mask_in, cells_in, owner_in,
    o_red, o_samp, o_gram, o_proj,
    mask, cell_row, own_row, raw_b, raw_g, raw_s, st, rate, other, gat, hot, slots,
    acc_p, picks, pbg, t0, t0r, t1, t1r, relay, w32, w16, w16r, hb, hr, mb, mr, acc_n, acc_f, fb, fr,
    lsem, ssem, rsem, hsem, tsem, gsem, wsem, qsem, msem, fsem, xsem,
):
    g = lax.axis_index("grid")
    m = lax.axis_index("mode")
    ny = nm // 2
    c = lax.rem(m, 2)
    y = m // 2
    right = lax.rem(y + 1, ny) * 2 + c
    left = lax.rem(y + ny - 1, ny) * 2 + c
    opp = lax.rem(y + 2, ny) * 2 + c
    sib = y * 2 + (1 - c)
    flip = 1 - 2 * c
    modes = basis.shape[1]
    snaps = state.shape[1]
    nrow = state.shape[2]
    ncol = state.shape[3]
    samp = cells_in.shape[1]
    nchunk = 2 * nrow

    half_col = ncol // 2
    loads = [
        pltpu.make_async_copy(basis.at[0, :, :, 0:half_col], raw_b.at[0, :, :, 0:half_col], lsem.at[0]),
        pltpu.make_async_copy(basis.at[0, :, :, half_col:ncol], raw_b.at[0, :, :, half_col:ncol], lsem.at[1]),
        pltpu.make_async_copy(basis.at[1], raw_b.at[1], lsem.at[2]),
        pltpu.make_async_copy(state.at[0], raw_s.at[0], lsem.at[3]),
        pltpu.make_async_copy(state.at[1], raw_s.at[1], lsem.at[4]),
    ]
    small = [
        pltpu.make_async_copy(mask_in, mask, lsem.at[5]),
        pltpu.make_async_copy(cells_in, cell_row, lsem.at[6]),
        pltpu.make_async_copy(owner_in, own_row, lsem.at[7]),
    ]

    barrier = pltpu.get_barrier_semaphore()
    for d in range(1, nm):
        pl.semaphore_signal(barrier, inc=1, device_id=(g, lax.rem(m + d, nm)), device_id_type=MESH)
    for d in range(1, ng):
        pl.semaphore_signal(barrier, inc=1, device_id=(lax.rem(g + d, ng), m), device_id_type=MESH)

    for load in loads[:3] + small:
        load.start()
    sent = []

    def push(src, dst, send_sem, recv_sem, device):
        copy = pltpu.make_async_remote_copy(
            src_ref=src, dst_ref=dst, send_sem=send_sem, recv_sem=recv_sem,
            device_id=device, device_id_type=MESH,
        )
        copy.start()
        sent.append(copy)

    def await_recv(dst, send_sem, recv_sem):
        pltpu.make_async_remote_copy(
            src_ref=dst, dst_ref=dst, send_sem=send_sem, recv_sem=recv_sem,
            device_id=(g, sib), device_id_type=MESH,
        ).wait_recv()

    pieces = [(0, 4, 0, half_col // 2), (0, 4, half_col // 2, half_col // 2)]
    pieces += [(k, 2, half_col, half_col) for k in (0, 2)]
    pieces += [(k, 1, 0, ncol) for k in (4, 5)]
    pieces += [(k, 1, col, half_col) for col in (0, half_col) for k in (6, 7)]
    npiece = len(pieces)
    seen = (m, right, left, opp)

    def slot(j, rel, owner):
        if j < 2:
            return raw_g.at[rel, j]
        if j < npiece:
            k, count, col, size = pieces[j]
            return gat.at[k : k + count, rel, :, col : col + size]
        return pbg.at[j - npiece, owner]

    def ag_send(j, rel, there, kind, to):
        source = slot(j, rel, seen[rel])
        if j < 2 and rel == 0:
            source = basis.at[0, :, :, pieces[j][2] : pieces[j][2] + pieces[j][3]]
        push(
            source, slot(j, there, seen[rel]),
            ssem.at[kind, j], rsem.at[there, c, j], (g, to),
        )

    def ag_recv(j, rel):
        await_recv(slot(j, rel, seen[rel]), ssem.at[0, j], rsem.at[rel, c, j])

    def start(j):
        ag_send(j, 0, 2, 0, right)
        ag_send(j, 0, 1, 1, left)

    def unpack(j, rel):
        if j < 2:
            first, count, col, size = pieces[j]
            gat[first : first + count, rel, :, col : col + size] = jnp.swapaxes(raw_g[rel, j], 0, 1)

    def near(j):
        for rel, kind in ((2, 4), (1, 5)):
            ag_recv(j, rel)
            if j >= npiece:
                ag_send(j, rel, rel, kind, sib)
            unpack(j, rel)

    def onward(j):
        if j % 2 == 0:
            ag_send(j, 2, 3, 3, right)
        else:
            ag_send(j, 1, 3, 3, left)

    def far(j):
        ag_recv(j, 3)
        if j >= npiece:
            ag_send(j, 3, 3, 6, sib)
        unpack(j, 3)

    def wait_sib(j):
        for rel in range(4):
            await_recv(pbg.at[j - npiece, seen[rel] + flip], ssem.at[0, j], rsem.at[rel, 1 - c, j])

    def project(j, acc, low, high):
        first, count, col, size = pieces[j]
        for k in range(first, first + count):
            s, r = k // nrow, k % nrow
            block = gat[k, low:high, :, col : col + size].reshape(acc.shape[0], size)
            both = jnp.concatenate(
                [
                    rate[r, s * snaps : (s + 1) * snaps, col : col + size],
                    other[r, s * snaps : (s + 1) * snaps, col : col + size],
                ],
                axis=0,
            )
            acc[...] += dot_nt(block, both)

    def project_near(j):
        project(j, acc_n, 0, 3)

    def project_far(j):
        project(j, acc_f, 3, 4)

    def split_basis(s, col, size):
        mine = jnp.swapaxes(raw_b[s, :, :, col : col + size], 0, 1)
        gat[pl.ds(s * nrow, nrow), 0, :, col : col + size] = mine
        rate[:, 2 * snaps + s * modes : 2 * snaps + (s + 1) * modes, col : col + size] = mine

    pl.semaphore_wait(barrier, nm - 1 + ng - 1)
    start(0)
    start(1)
    loads[0].wait()
    split_basis(0, 0, half_col)
    loads[1].wait()
    split_basis(0, half_col, half_col)
    start(2)
    start(3)
    loads[2].wait()
    loads[3].start()
    loads[4].start()
    split_basis(1, 0, ncol)
    start(4)
    start(5)

    step = 16
    loads[3].wait()

    def split_s(i, carry):
        rows = pl.ds(pl.multiple_of(i * step, step), step)
        st[pl.ds(1, nrow), rows] = jnp.swapaxes(raw_s[0, rows], 0, 1)
        return carry

    lax.fori_loop(0, snaps // step, split_s, 0)
    up_dev = lax.rem(g + 1, ng)
    down_dev = lax.rem(g + ng - 1, ng)
    push(st.at[nrow], st.at[0], hsem.at[0], hsem.at[1], (up_dev, m))
    push(st.at[1], st.at[nrow + 1], hsem.at[2], hsem.at[3], (down_dev, m))
    loads[4].wait()

    def split_b(i, carry):
        rows = pl.ds(pl.multiple_of(i * step, step), step)
        high = pl.ds(pl.multiple_of(i * step + snaps, step), step)
        rate[:, high] = jnp.swapaxes(raw_s[1, rows], 0, 1)
        return carry

    lax.fori_loop(0, snaps // step, split_b, 0)

    for load in small:
        load.wait()
    lane = lax.broadcasted_iota(jnp.int32, (step, ncol), 1)

    def rates(r):
        film = jnp.broadcast_to(mask[pl.ds(r, 1), :].astype(F32), (step, ncol))
        up_on = jnp.where(jnp.logical_and(r == 0, g == 0), 0.0, 1.0).astype(F32)
        down_on = jnp.where(jnp.logical_and(r == nrow - 1, g == ng - 1), 0.0, 1.0).astype(F32)

        def body(i, carry):
            rows = pl.ds(pl.multiple_of(i * step, step), step)
            high = pl.ds(pl.multiple_of(i * step + snaps, step), step)
            sub = st[r + 1, rows].astype(F32)
            up = st[r, rows].astype(F32) * up_on
            down = st[r + 2, rows].astype(F32) * down_on
            bio = rate[r, high].astype(F32)
            before = jnp.where(lane == 0, 0.0, pltpu.roll(sub, 1, 1))
            after = jnp.where(lane == ncol - 1, 0.0, pltpu.roll(sub, ncol - 1, 1))
            lap = down + up + after + before - 4.0 * sub
            taken = bio * (sub / (0.5 + sub))
            rate[r, rows] = ((1.0 - 0.2 * film) * lap - 2.0 * taken).astype(BF16)
            rate[r, high] = (film * (taken - 0.1 * bio)).astype(BF16)
            return carry

        lax.fori_loop(0, snaps // step, body, 0)
        push(rate.at[r, 0 : 2 * snaps], other.at[r], xsem.at[0, r], xsem.at[1, r], (g, sib))

    cells = cell_row[...].astype(F32)
    part_rows = 512

    def pick(r):
        def build(i, carry):
            base = (r * ncol + i * part_rows).astype(F32)
            number = lax.broadcasted_iota(jnp.int32, (part_rows, samp), 0).astype(F32) + base
            rows = pl.ds(pl.multiple_of(i * part_rows, part_rows), part_rows)
            hot[rows] = jnp.where(number == cells, 1.0, 0.0).astype(BF16)
            return carry

        lax.fori_loop(0, ncol // part_rows, build, 0)
        acc_p[...] += jnp.dot(rate[r], hot[...], preferred_element_type=F32)

    acc_p[...] = jnp.zeros(acc_p.shape, F32)
    acc_n[...] = jnp.zeros(acc_n.shape, F32)
    acc_f[...] = jnp.zeros(acc_f.shape, F32)
    rates(1)
    near(0)
    rates(2)
    pick(1)
    near(1)
    pick(2)
    near(2)

    ii = lax.broadcasted_iota(jnp.int32, (samp, samp), 0)
    jj = lax.broadcasted_iota(jnp.int32, (samp, samp), 1)
    own = jnp.broadcast_to(own_row[...].astype(F32), (samp, samp))
    own_col = jnp.sum(jnp.where(ii == jj, own, 0.0), axis=1, keepdims=True)
    same = jnp.logical_and(own == own_col, ii < jj)
    rank = jnp.sum(jnp.where(same, 1.0, 0.0), axis=0, keepdims=True)
    own_f = own_row[...].astype(F32)
    own_hi = jnp.floor(own_f * (1.0 / nm))
    own_lo = own_f - own_hi * nm
    key = own_f * 8.0 + rank
    for gg in range(ng):
        number = lax.broadcasted_iota(jnp.int32, (8 * nm, samp), 0).astype(F32) + float(gg * 8 * nm)
        slots[gg] = jnp.where(number == key, 1.0, 0.0).astype(BF16)
    key = jnp.where(own_lo == m.astype(F32), own_hi * 8.0 + rank, -1.0)
    number = lax.broadcasted_iota(jnp.int32, (8 * ng, samp), 0).astype(F32)
    mine = jnp.where(number == key, 1.0, 0.0).astype(BF16)

    near(3)
    for j in range(4):
        onward(j)
    await_recv(st.at[0], hsem.at[0], hsem.at[1])
    await_recv(st.at[nrow + 1], hsem.at[2], hsem.at[3])
    rates(0)
    near(4)
    pick(0)
    rates(nrow - 1)
    pick(nrow - 1)
    picks[...] = acc_p[...].astype(BF16)
    for s in range(2):
        pbg[s, m] = picks[2 * snaps + s * modes : 2 * snaps + (s + 1) * modes, :]
    picked = (npiece, npiece + 1)
    for j in picked:
        start(j)
    start(6)
    start(7)
    for j in picked:
        ag_send(j, 0, 0, 2, sib)
    rows = dot_nt(slots[...].reshape(8 * nm * ng, samp), picks[0 : 2 * snaps, :])
    t0[...] = rows.astype(BF16).reshape(t0.shape)
    for d in range(1, ng):
        to = lax.rem(g + d, ng)
        push(t0.at[to], t0r.at[g], gsem.at[0, d], gsem.at[1, d], (to, m))
    t0r[g] = t0[g]

    def row_send(src, dst, n, origin, to):
        push(src, dst, tsem.at[0, n], tsem.at[1, origin], (g, to))

    def row_recv(dst, origin):
        await_recv(dst, tsem.at[0, 0], tsem.at[1, origin])

    near(5)
    for r in range(nrow):
        await_recv(other.at[r], xsem.at[0, r], xsem.at[1, r])
    for j in range(6):
        project_near(j)
    far(0)
    far(1)
    for j in picked:
        near(j)
        onward(j)
    start(8)
    start(9)
    for j in range(4, 6):
        onward(j)
    project_far(0)
    project_far(1)
    near(6)
    onward(6)
    near(7)
    onward(7)
    for j in picked:
        far(j)
    for j in picked:
        wait_sib(j)

    hyper = jnp.zeros((nm * modes, snaps), F32)
    gram = jnp.zeros((nm * modes, modes), F32)
    for s in range(2):
        all_modes = pbg[s].reshape(nm * modes, samp)
        hyper = hyper + dot_nt(all_modes, picks[s * snaps : (s + 1) * snaps, :])
        gram = gram + dot_nt(all_modes, pbg[s, m])
        w32[:, 8 * s : 8 * s + 8, :] = dot_nt(mine, all_modes).reshape(ng, 8, nm * modes)
    hb[...] = jnp.zeros(hb.shape, F32)
    hb[:, :, 0:128] = (weight * hyper).reshape(ng, 16, snaps)
    hb[:, :, 128 : 128 + modes] = (weight * gram).reshape(ng, 16, modes)
    for d in range(1, ng):
        to = lax.rem(g + d, ng)
        push(hb.at[to], hr.at[g], qsem.at[0, d], qsem.at[1, d], (to, m))
    hr[g] = hb[g]

    w16[...] = w32[...].astype(BF16)
    for d in range(1, ng):
        to = lax.rem(g + d, ng)
        push(w16.at[to], w16r.at[g], wsem.at[0, d], wsem.at[1, d], (to, m))
    w16r[g] = w16[g]

    for d in range(1, ng):
        frm = lax.rem(g + ng - d, ng)
        await_recv(t0r.at[frm], gsem.at[0, d], gsem.at[1, d])
    for mm in range(nm):
        t1[mm] = t0r[...].astype(F32)[:, 8 * mm : 8 * mm + 8, :].reshape(ng * 8, 2 * snaps).astype(BF16)
    near(8)
    onward(8)
    near(9)
    onward(9)
    settled = len(sent) - 6
    row_send(t1.at[opp], relay.at[0], 0, nm, right)
    row_send(t1.at[opp + flip], relay.at[1], 1, nm + 1, left)
    row_send(t1.at[right], t1r.at[m], 2, m, right)
    row_send(t1.at[left], t1r.at[m], 3, m, left)
    row_send(t1.at[right + flip], t1r.at[m], 4, m, right + flip)
    row_send(t1.at[left + flip], t1r.at[m], 5, m, left + flip)
    row_send(t1.at[sib], t1r.at[m], 6, m, sib)
    t1r[m] = t1[m]
    for j in range(6, 10):
        project_near(j)

    def sums(acc, rels):
        for n, rel in enumerate(rels):
            for h in range(2):
                to = seen[rel] // 2 * (ng // ny) + 2 * c + h
                for t in range(2):
                    low = modes * n + fb.shape[3] * h
                    fb[t, rel, h] = acc[low : low + fb.shape[3], t * snaps : (t + 1) * snaps]
                    copy = pltpu.make_async_remote_copy(
                        src_ref=fb.at[t, rel, h], dst_ref=fr.at[g],
                        send_sem=fsem.at[0, t * 8 + rel * 2 + h], recv_sem=fsem.at[1, g],
                        device_id=(to, sib if t else m), device_id_type=MESH,
                    )
                    if t:
                        copy.start()
                        sent.append(copy)
                    else:
                        pl.when(to != g)(copy.start)
                        last.append((to, copy))

                        @pl.when(to == g)
                        def _():
                            fr[g] = fb[t, rel, h]

    last = []
    sums(acc_n, range(3))
    far(2)
    far(3)
    project_far(2)
    project_far(3)
    for d in range(1, ng):
        frm = lax.rem(g + ng - d, ng)
        await_recv(w16r.at[frm], wsem.at[0, d], wsem.at[1, d])
    for s in range(2):
        part = w16r[...].astype(F32)[:, 8 * s : 8 * s + 8, :].reshape(ng * 8, nm * modes)
        o_samp[0, :, s * nm * modes : (s + 1) * nm * modes] = part.astype(BF16)
    for d in range(1, ng):
        frm = lax.rem(g + ng - d, ng)
        await_recv(hr.at[frm], qsem.at[0, d], qsem.at[1, d])
    total = jnp.sum(hr[...], axis=0)
    mb[...] = jnp.zeros(mb.shape, F32)
    for mm in range(nm):
        mb[mm, 0:2, :] = total[2 * mm : 2 * mm + 2, :]
    for d in range(1, nm):
        to = lax.rem(m + d, nm)
        push(mb.at[to], mr.at[m], msem.at[0, d], msem.at[1, d], (g, to))
    mr[m] = mb[m]
    far(4)
    far(5)
    project_far(4)
    project_far(5)
    for copy in sent[:settled]:
        copy.wait_send()
    del sent[:settled]
    far(6)
    far(7)
    project_far(6)
    project_far(7)
    far(8)
    far(9)
    row_recv(relay.at[0], nm)
    row_send(relay.at[0], t1r.at[left], 7, left, right)
    row_recv(relay.at[1], nm + 1)
    row_send(relay.at[1], t1r.at[right], 8, right, left + flip)
    project_far(8)
    project_far(9)
    sums(acc_f, range(3, 4))
    for frm in (sib, right, right + flip, left, left + flip, opp, opp + flip):
        row_recv(t1r.at[frm], frm)
    for mm in range(nm):
        for s in range(2):
            col = 2 * nm * modes + s * nm * snaps + mm * snaps
            o_samp[0, :, col : col + snaps] = t1r[mm, :, s * snaps : (s + 1) * snaps]
    for d in range(1, nm):
        frm = lax.rem(m + nm - d, nm)
        await_recv(mr.at[frm], msem.at[0, d], msem.at[1, d])
    for mm in range(nm):
        o_proj[:, mm * snaps : (mm + 1) * snaps] = mr[mm, 0:2, 0:snaps]
        o_gram[:, mm * modes : (mm + 1) * modes] = mr[mm, 0:2, 128 : 128 + modes]
    mine_core = lax.rem(g // 2, 2) == c
    for frm in range(ng):

        @pl.when(jnp.logical_or(frm != g, jnp.logical_not(mine_core)))
        def _():
            await_recv(fr.at[frm], fsem.at[0, frm], fsem.at[1, frm])

    o_red[...] = jnp.sum(fr[...], axis=0)
    for copy in sent:
        copy.wait_send()
    for to, copy in last:
        pl.when(to != g)(copy.wait_send)


def finish(*refs):
    for source, target in zip(refs[:4], refs[4:]):
        target[...] = source[...]


def per_device(ng, nm, state, film_mask, basis, sample_cells, owner):
    modes, snaps = basis.shape[1], state.shape[1]
    nrow, ncol = state.shape[2:]
    samp = sample_cells.shape[1]
    nchunk = 2 * nrow
    width = 2 * nm * (modes + snaps)
    dma = pltpu.SemaphoreType.DMA
    vmem = pl.BlockSpec(memory_space=pltpu.VMEM)
    hbm = pl.BlockSpec(memory_space=pl.ANY)
    outs = pl.pallas_call(
        functools.partial(kernel, ng, nm, nrow * ncol / samp),
        out_shape=(
            pltpu.VMEM((nm * modes // ng, snaps), F32),
            pltpu.VMEM((1, ng * 8, width), BF16),
            pltpu.VMEM((2, nm * modes), F32),
            pltpu.VMEM((2, nm * snaps), F32),
        ),
        in_specs=[hbm] * 5,
        out_specs=(vmem, vmem, vmem, vmem),
        scratch_shapes=[
            pltpu.VMEM((nrow, ncol), jnp.int32),
            pltpu.VMEM((1, samp), jnp.int32),
            pltpu.VMEM((1, samp), jnp.int32),
            pltpu.VMEM((2, modes, nrow, ncol), BF16),
            pltpu.VMEM((nm // 2, 2, modes, nrow, ncol // 4), BF16),
            pltpu.VMEM((2, snaps, nrow, ncol), BF16),
            pltpu.VMEM((nrow + 2, snaps, ncol), BF16),
            pltpu.VMEM((nrow, 2 * (snaps + modes), ncol), BF16),
            pltpu.VMEM((nrow, 2 * snaps, ncol), BF16),
            pltpu.VMEM((nchunk, nm // 2, modes, ncol), BF16),
            pltpu.VMEM((ncol, samp), BF16),
            pltpu.VMEM((ng, 8 * nm, samp), BF16),
            pltpu.VMEM((2 * (snaps + modes), samp), F32),
            pltpu.VMEM((2 * (snaps + modes), samp), BF16),
            pltpu.VMEM((2, nm, modes, samp), BF16),
            pltpu.VMEM((ng, 8 * nm, 2 * snaps), BF16),
            pltpu.VMEM((ng, 8 * nm, 2 * snaps), BF16),
            pltpu.VMEM((nm, 8 * ng, 2 * snaps), BF16),
            pltpu.VMEM((nm, 8 * ng, 2 * snaps), BF16),
            pltpu.VMEM((2, 128, 2 * snaps), BF16),
            pltpu.VMEM((ng, 16, nm * modes), F32),
            pltpu.VMEM((ng, 16, nm * modes), BF16),
            pltpu.VMEM((ng, 16, nm * modes), BF16),
            pltpu.VMEM((ng, 16, 256), F32),
            pltpu.VMEM((ng, 16, 256), F32),
            pltpu.VMEM((nm, 8, 256), F32),
            pltpu.VMEM((nm, 8, 256), F32),
            pltpu.VMEM((3 * modes, 2 * snaps), F32),
            pltpu.VMEM((modes, 2 * snaps), F32),
            pltpu.VMEM((2, nm // 2, 2, nm * modes // ng, snaps), F32),
            pltpu.VMEM((ng, nm * modes // ng, snaps), F32),
            dma((8,)),
            dma((7, nchunk + 4)),
            dma((4, 2, nchunk + 4)),
            dma((4,)),
            dma((2, nm + 2)),
            dma((2, ng)),
            dma((2, ng)),
            dma((2, ng)),
            dma((2, nm)),
            dma((2, ng)),
            dma((2, nrow)),
        ],
        compiler_params=pltpu.CompilerParams(
            collective_id=0, has_side_effects=True, vmem_limit_bytes=59 << 20
        ),
    )(state, basis, film_mask, sample_cells, owner.reshape(1, samp))
    return pl.pallas_call(
        finish,
        out_shape=tuple(jax.ShapeDtypeStruct(o.shape, o.dtype) for o in outs),
        in_specs=[vmem] * 4,
        out_specs=(vmem,) * 4,
    )(*[pltpu.with_memory_space_constraint(o, pltpu.VMEM) for o in outs])


def solution(mesh):
    in_specs = (
        P(None, "mode", "grid", None),
        P("grid", None),
        P(None, "mode", "grid", None),
        P("grid", None),
        P("grid", None, None),
    )
    out_specs = (
        P("grid", "mode"),
        P(("grid", "mode"), None, None),
        P(("grid", "mode"), None),
        P(("grid", "mode"), None),
    )
    return jax.shard_map(
        functools.partial(per_device, mesh.shape["grid"], mesh.shape["mode"]),
        mesh=mesh, in_specs=in_specs, out_specs=out_specs, check_vma=False,
    )
```

```python
import functools

import jax
import jax.numpy as jnp
from jax import lax
from jax.experimental import pallas as pl
from jax.experimental.pallas import tpu as pltpu
from jax.sharding import PartitionSpec as P

MESH = pl.DeviceIdType.MESH
F32 = jnp.float32
BF16 = jnp.bfloat16


def dot_nt(a, b):
    return lax.dot_general(a, b, (((1,), (1,)), ((), ())), preferred_element_type=F32)


def kernel(
    ng, nm, weight,
    state, basis, mask_in, cells_in, owner_in,
    o_red, o_samp, o_gram, o_proj,
    mask, cell_row, own_row, raw_b, raw_g, raw_s, st, rate, other, gat, hot, slots,
    acc_p, picks, pbg, t0, t0r, t1, t1r, relay, w32, w16, w16r, hb, hr, mb, mr, acc_n, acc_f, fb, fr,
    lsem, ssem, rsem, hsem, tsem, gsem, wsem, qsem, msem, fsem, xsem, known,
):
    g = lax.axis_index("grid")
    m = lax.axis_index("mode")
    ny = nm // 2
    c = lax.rem(m, 2)
    y = m // 2
    right = lax.rem(y + 1, ny) * 2 + c
    left = lax.rem(y + ny - 1, ny) * 2 + c
    opp = lax.rem(y + 2, ny) * 2 + c
    sib = y * 2 + (1 - c)
    flip = 1 - 2 * c
    modes = basis.shape[1]
    snaps = state.shape[1]
    nrow = state.shape[2]
    ncol = state.shape[3]
    samp = cells_in.shape[1]
    nchunk = 2 * nrow

    half_col = ncol // 2
    loads = [
        pltpu.make_async_copy(basis.at[0, :, :, 0:half_col], raw_b.at[0, :, :, 0:half_col], lsem.at[0]),
        pltpu.make_async_copy(basis.at[0, :, :, half_col:ncol], raw_b.at[0, :, :, half_col:ncol], lsem.at[1]),
        pltpu.make_async_copy(basis.at[1], raw_b.at[1], lsem.at[2]),
        pltpu.make_async_copy(state.at[0], raw_s.at[0], lsem.at[3]),
        pltpu.make_async_copy(state.at[1], raw_s.at[1], lsem.at[4]),
    ]
    small = [
        pltpu.make_async_copy(mask_in, mask, lsem.at[5]),
        pltpu.make_async_copy(cells_in, cell_row, lsem.at[6]),
        pltpu.make_async_copy(owner_in, own_row, lsem.at[7]),
    ]

    up_dev = lax.rem(g + 1, ng)
    down_dev = lax.rem(g + ng - 1, ng)
    around = [(g, right), (g, left), (g, sib), (up_dev, m), (down_dev, m)]
    barrier = pltpu.get_barrier_semaphore()
    for dev in around:
        pl.semaphore_signal(barrier, inc=1, device_id=dev, device_id_type=MESH)
    rounds = [around]
    rounds.append([(lax.rem(g + 2, ng), m), (lax.rem(g + ng - 2, ng), m), (g, sib)])
    rounds.append([(lax.rem(g + 4, ng), m), (lax.rem(g + ng - 4, ng), m)])

    def announce(n):
        for dev in rounds[n]:
            pl.semaphore_signal(known.at[n], inc=1, device_id=dev, device_id_type=MESH)

    def heard(n):
        pl.semaphore_wait(known.at[n], len(rounds[n]))

    for load in loads[:3] + small:
        load.start()
    sent = []

    def push(src, dst, send_sem, recv_sem, device):
        copy = pltpu.make_async_remote_copy(
            src_ref=src, dst_ref=dst, send_sem=send_sem, recv_sem=recv_sem,
            device_id=device, device_id_type=MESH,
        )
        copy.start()
        sent.append(copy)

    def await_recv(dst, send_sem, recv_sem):
        pltpu.make_async_remote_copy(
            src_ref=dst, dst_ref=dst, send_sem=send_sem, recv_sem=recv_sem,
            device_id=(g, sib), device_id_type=MESH,
        ).wait_recv()

    pieces = [(0, 4, 0, half_col // 2), (0, 4, half_col // 2, half_col // 2)]
    pieces += [(k, 2, half_col, half_col) for k in (0, 2)]
    pieces += [(k, 1, 0, ncol) for k in (4, 5)]
    pieces += [(k, 1, col, half_col) for col in (0, half_col) for k in (6, 7)]
    npiece = len(pieces)
    seen = (m, right, left, opp)

    def slot(j, rel, owner):
        if j < 2:
            return raw_g.at[rel, j]
        if j < npiece:
            k, count, col, size = pieces[j]
            return gat.at[k : k + count, rel, :, col : col + size]
        return pbg.at[j - npiece, owner]

    def ag_send(j, rel, there, kind, to):
        source = slot(j, rel, seen[rel])
        if j < 2 and rel == 0:
            source = basis.at[0, :, :, pieces[j][2] : pieces[j][2] + pieces[j][3]]
        push(
            source, slot(j, there, seen[rel]),
            ssem.at[kind, j], rsem.at[there, c, j], (g, to),
        )

    def ag_recv(j, rel):
        await_recv(slot(j, rel, seen[rel]), ssem.at[0, j], rsem.at[rel, c, j])

    def start(j):
        ag_send(j, 0, 2, 0, right)
        ag_send(j, 0, 1, 1, left)

    def unpack(j, rel):
        if j < 2:
            first, count, col, size = pieces[j]
            gat[first : first + count, rel, :, col : col + size] = jnp.swapaxes(raw_g[rel, j], 0, 1)

    def near(j):
        for rel, kind in ((2, 4), (1, 5)):
            ag_recv(j, rel)
            if j >= npiece:
                ag_send(j, rel, rel, kind, sib)
            unpack(j, rel)

    def onward(j):
        if j % 2 == 0:
            ag_send(j, 2, 3, 3, right)
        else:
            ag_send(j, 1, 3, 3, left)

    def far(j):
        ag_recv(j, 3)
        if j >= npiece:
            ag_send(j, 3, 3, 6, sib)
        unpack(j, 3)

    def wait_sib(j):
        for rel in range(4):
            await_recv(pbg.at[j - npiece, seen[rel] + flip], ssem.at[0, j], rsem.at[rel, 1 - c, j])

    def project(j, acc, low, high):
        first, count, col, size = pieces[j]
        for k in range(first, first + count):
            s, r = k // nrow, k % nrow
            block = gat[k, low:high, :, col : col + size].reshape(acc.shape[0], size)
            both = jnp.concatenate(
                [
                    rate[r, s * snaps : (s + 1) * snaps, col : col + size],
                    other[r, s * snaps : (s + 1) * snaps, col : col + size],
                ],
                axis=0,
            )
            acc[...] += dot_nt(block, both)

    def project_near(j):
        project(j, acc_n, 0, 3)

    def project_far(j):
        project(j, acc_f, 3, 4)

    def split_basis(s, col, size):
        mine = jnp.swapaxes(raw_b[s, :, :, col : col + size], 0, 1)
        gat[pl.ds(s * nrow, nrow), 0, :, col : col + size] = mine
        rate[:, 2 * snaps + s * modes : 2 * snaps + (s + 1) * modes, col : col + size] = mine

    pl.semaphore_wait(barrier, len(around))
    start(0)
    start(1)
    announce(0)
    loads[0].wait()
    split_basis(0, 0, half_col)
    loads[1].wait()
    split_basis(0, half_col, half_col)
    start(2)
    start(3)
    loads[2].wait()
    loads[3].start()
    loads[4].start()
    split_basis(1, 0, ncol)
    start(4)
    start(5)

    step = 16
    loads[3].wait()

    def split_s(i, carry):
        rows = pl.ds(pl.multiple_of(i * step, step), step)
        st[pl.ds(1, nrow), rows] = jnp.swapaxes(raw_s[0, rows], 0, 1)
        return carry

    lax.fori_loop(0, snaps // step, split_s, 0)
    heard(0)
    announce(1)
    push(st.at[nrow], st.at[0], hsem.at[0], hsem.at[1], (up_dev, m))
    push(st.at[1], st.at[nrow + 1], hsem.at[2], hsem.at[3], (down_dev, m))
    loads[4].wait()

    def split_b(i, carry):
        rows = pl.ds(pl.multiple_of(i * step, step), step)
        high = pl.ds(pl.multiple_of(i * step + snaps, step), step)
        rate[:, high] = jnp.swapaxes(raw_s[1, rows], 0, 1)
        return carry

    lax.fori_loop(0, snaps // step, split_b, 0)

    for load in small:
        load.wait()
    lane = lax.broadcasted_iota(jnp.int32, (step, ncol), 1)

    def rates(r):
        film = jnp.broadcast_to(mask[pl.ds(r, 1), :].astype(F32), (step, ncol))
        up_on = jnp.where(jnp.logical_and(r == 0, g == 0), 0.0, 1.0).astype(F32)
        down_on = jnp.where(jnp.logical_and(r == nrow - 1, g == ng - 1), 0.0, 1.0).astype(F32)

        def body(i, carry):
            rows = pl.ds(pl.multiple_of(i * step, step), step)
            high = pl.ds(pl.multiple_of(i * step + snaps, step), step)
            sub = st[r + 1, rows].astype(F32)
            up = st[r, rows].astype(F32) * up_on
            down = st[r + 2, rows].astype(F32) * down_on
            bio = rate[r, high].astype(F32)
            before = jnp.where(lane == 0, 0.0, pltpu.roll(sub, 1, 1))
            after = jnp.where(lane == ncol - 1, 0.0, pltpu.roll(sub, ncol - 1, 1))
            lap = down + up + after + before - 4.0 * sub
            taken = bio * (sub / (0.5 + sub))
            rate[r, rows] = ((1.0 - 0.2 * film) * lap - 2.0 * taken).astype(BF16)
            rate[r, high] = (film * (taken - 0.1 * bio)).astype(BF16)
            return carry

        lax.fori_loop(0, snaps // step, body, 0)
        push(rate.at[r, 0 : 2 * snaps], other.at[r], xsem.at[0, r], xsem.at[1, r], (g, sib))

    cells = cell_row[...].astype(F32)
    part_rows = 512

    def pick(r):
        def build(i, carry):
            base = (r * ncol + i * part_rows).astype(F32)
            number = lax.broadcasted_iota(jnp.int32, (part_rows, samp), 0).astype(F32) + base
            rows = pl.ds(pl.multiple_of(i * part_rows, part_rows), part_rows)
            hot[rows] = jnp.where(number == cells, 1.0, 0.0).astype(BF16)
            return carry

        lax.fori_loop(0, ncol // part_rows, build, 0)
        acc_p[...] += jnp.dot(rate[r], hot[...], preferred_element_type=F32)

    acc_p[...] = jnp.zeros(acc_p.shape, F32)
    acc_n[...] = jnp.zeros(acc_n.shape, F32)
    acc_f[...] = jnp.zeros(acc_f.shape, F32)
    rates(1)
    heard(1)
    announce(2)
    near(0)
    rates(2)
    heard(2)
    pick(1)
    near(1)
    pick(2)
    near(2)

    ii = lax.broadcasted_iota(jnp.int32, (samp, samp), 0)
    jj = lax.broadcasted_iota(jnp.int32, (samp, samp), 1)
    own = jnp.broadcast_to(own_row[...].astype(F32), (samp, samp))
    own_col = jnp.sum(jnp.where(ii == jj, own, 0.0), axis=1, keepdims=True)
    same = jnp.logical_and(own == own_col, ii < jj)
    rank = jnp.sum(jnp.where(same, 1.0, 0.0), axis=0, keepdims=True)
    own_f = own_row[...].astype(F32)
    own_hi = jnp.floor(own_f * (1.0 / nm))
    own_lo = own_f - own_hi * nm
    key = own_f * 8.0 + rank
    for gg in range(ng):
        number = lax.broadcasted_iota(jnp.int32, (8 * nm, samp), 0).astype(F32) + float(gg * 8 * nm)
        slots[gg] = jnp.where(number == key, 1.0, 0.0).astype(BF16)
    key = jnp.where(own_lo == m.astype(F32), own_hi * 8.0 + rank, -1.0)
    number = lax.broadcasted_iota(jnp.int32, (8 * ng, samp), 0).astype(F32)
    mine = jnp.where(number == key, 1.0, 0.0).astype(BF16)

    near(3)
    for j in range(4):
        onward(j)
    await_recv(st.at[0], hsem.at[0], hsem.at[1])
    await_recv(st.at[nrow + 1], hsem.at[2], hsem.at[3])
    rates(0)
    near(4)
    pick(0)
    rates(nrow - 1)
    pick(nrow - 1)
    picks[...] = acc_p[...].astype(BF16)
    for s in range(2):
        pbg[s, m] = picks[2 * snaps + s * modes : 2 * snaps + (s + 1) * modes, :]
    picked = (npiece, npiece + 1)
    for j in picked:
        start(j)
    start(6)
    start(7)
    for j in picked:
        ag_send(j, 0, 0, 2, sib)
    rows = dot_nt(slots[...].reshape(8 * nm * ng, samp), picks[0 : 2 * snaps, :])
    t0[...] = rows.astype(BF16).reshape(t0.shape)
    for d in range(1, ng):
        to = lax.rem(g + d, ng)
        push(t0.at[to], t0r.at[g], gsem.at[0, d], gsem.at[1, d], (to, m))
    t0r[g] = t0[g]

    def row_send(src, dst, n, origin, to):
        push(src, dst, tsem.at[0, n], tsem.at[1, origin], (g, to))

    def row_recv(dst, origin):
        await_recv(dst, tsem.at[0, 0], tsem.at[1, origin])

    near(5)
    for r in range(nrow):
        await_recv(other.at[r], xsem.at[0, r], xsem.at[1, r])
    for j in range(6):
        project_near(j)
    far(0)
    far(1)
    for j in picked:
        near(j)
        onward(j)
    start(8)
    start(9)
    for j in range(4, 6):
        onward(j)
    project_far(0)
    project_far(1)
    near(6)
    onward(6)
    near(7)
    onward(7)
    for j in picked:
        far(j)
    for j in picked:
        wait_sib(j)

    hyper = jnp.zeros((nm * modes, snaps), F32)
    gram = jnp.zeros((nm * modes, modes), F32)
    for s in range(2):
        all_modes = pbg[s].reshape(nm * modes, samp)
        hyper = hyper + dot_nt(all_modes, picks[s * snaps : (s + 1) * snaps, :])
        gram = gram + dot_nt(all_modes, pbg[s, m])
        w32[:, 8 * s : 8 * s + 8, :] = dot_nt(mine, all_modes).reshape(ng, 8, nm * modes)
    hb[...] = jnp.zeros(hb.shape, F32)
    hb[:, :, 0:128] = (weight * hyper).reshape(ng, 16, snaps)
    hb[:, :, 128 : 128 + modes] = (weight * gram).reshape(ng, 16, modes)
    for d in range(1, ng):
        to = lax.rem(g + d, ng)
        push(hb.at[to], hr.at[g], qsem.at[0, d], qsem.at[1, d], (to, m))
    hr[g] = hb[g]

    w16[...] = w32[...].astype(BF16)
    for d in range(1, ng):
        to = lax.rem(g + d, ng)
        push(w16.at[to], w16r.at[g], wsem.at[0, d], wsem.at[1, d], (to, m))
    w16r[g] = w16[g]

    for d in range(1, ng):
        frm = lax.rem(g + ng - d, ng)
        await_recv(t0r.at[frm], gsem.at[0, d], gsem.at[1, d])
    for mm in range(nm):
        t1[mm] = t0r[...].astype(F32)[:, 8 * mm : 8 * mm + 8, :].reshape(ng * 8, 2 * snaps).astype(BF16)
    near(8)
    onward(8)
    near(9)
    onward(9)
    settled = len(sent) - 6
    row_send(t1.at[opp], relay.at[0], 0, nm, right)
    row_send(t1.at[opp + flip], relay.at[1], 1, nm + 1, left)
    row_send(t1.at[right], t1r.at[m], 2, m, right)
    row_send(t1.at[left], t1r.at[m], 3, m, left)
    row_send(t1.at[right + flip], t1r.at[m], 4, m, right + flip)
    row_send(t1.at[left + flip], t1r.at[m], 5, m, left + flip)
    row_send(t1.at[sib], t1r.at[m], 6, m, sib)
    t1r[m] = t1[m]
    for j in range(6, 10):
        project_near(j)

    def sums(acc, rels):
        for n, rel in enumerate(rels):
            for h in range(2):
                to = seen[rel] // 2 * (ng // ny) + 2 * c + h
                for t in range(2):
                    low = modes * n + fb.shape[3] * h
                    fb[t, rel, h] = acc[low : low + fb.shape[3], t * snaps : (t + 1) * snaps]
                    copy = pltpu.make_async_remote_copy(
                        src_ref=fb.at[t, rel, h], dst_ref=fr.at[g],
                        send_sem=fsem.at[0, t * 8 + rel * 2 + h], recv_sem=fsem.at[1, g],
                        device_id=(to, sib if t else m), device_id_type=MESH,
                    )
                    if t:
                        copy.start()
                        sent.append(copy)
                    else:
                        pl.when(to != g)(copy.start)
                        last.append((to, copy))

                        @pl.when(to == g)
                        def _():
                            fr[g] = fb[t, rel, h]

    last = []
    sums(acc_n, range(3))
    far(2)
    far(3)
    project_far(2)
    project_far(3)
    for d in range(1, ng):
        frm = lax.rem(g + ng - d, ng)
        await_recv(w16r.at[frm], wsem.at[0, d], wsem.at[1, d])
    for s in range(2):
        part = w16r[...].astype(F32)[:, 8 * s : 8 * s + 8, :].reshape(ng * 8, nm * modes)
        o_samp[0, :, s * nm * modes : (s + 1) * nm * modes] = part.astype(BF16)
    for d in range(1, ng):
        frm = lax.rem(g + ng - d, ng)
        await_recv(hr.at[frm], qsem.at[0, d], qsem.at[1, d])
    total = jnp.sum(hr[...], axis=0)
    mb[...] = jnp.zeros(mb.shape, F32)
    for mm in range(nm):
        mb[mm, 0:2, :] = total[2 * mm : 2 * mm + 2, :]
    for d in range(1, nm):
        to = lax.rem(m + d, nm)
        push(mb.at[to], mr.at[m], msem.at[0, d], msem.at[1, d], (g, to))
    mr[m] = mb[m]
    far(4)
    far(5)
    project_far(4)
    project_far(5)
    for copy in sent[:settled]:
        copy.wait_send()
    del sent[:settled]
    far(6)
    far(7)
    project_far(6)
    project_far(7)
    far(8)
    far(9)
    row_recv(relay.at[0], nm)
    row_send(relay.at[0], t1r.at[left], 7, left, right)
    row_recv(relay.at[1], nm + 1)
    row_send(relay.at[1], t1r.at[right], 8, right, left + flip)
    project_far(8)
    project_far(9)
    sums(acc_f, range(3, 4))
    def place(frm):
        for s in range(2):
            col = pl.multiple_of(2 * nm * modes + s * nm * snaps + frm * snaps, 128)
            o_samp[0, :, pl.ds(col, snaps)] = t1r[frm, :, s * snaps : (s + 1) * snaps]

    place(m)
    row_recv(t1r.at[sib], sib)
    place(sib)
    for copy in sent:
        copy.wait_send()
    for to, copy in last:
        pl.when(to != g)(copy.wait_send)
    for frm in (right, right + flip, left, left + flip):
        row_recv(t1r.at[frm], frm)
        place(frm)
    mine_core = lax.rem(g // 2, 2) == c
    for frm in range(ng):

        @pl.when(jnp.logical_or(frm != g, jnp.logical_not(mine_core)))
        def _():
            await_recv(fr.at[frm], fsem.at[0, frm], fsem.at[1, frm])

    o_red[...] = jnp.sum(fr[...], axis=0)
    for frm in (opp, opp + flip):
        row_recv(t1r.at[frm], frm)
        place(frm)
    for d in range(1, nm):
        frm = lax.rem(m + nm - d, nm)
        await_recv(mr.at[frm], msem.at[0, d], msem.at[1, d])
    for mm in range(nm):
        o_proj[:, mm * snaps : (mm + 1) * snaps] = mr[mm, 0:2, 0:snaps]
        o_gram[:, mm * modes : (mm + 1) * modes] = mr[mm, 0:2, 128 : 128 + modes]


def finish(*refs):
    for source, target in zip(refs[:4], refs[4:]):
        target[...] = source[...]


def per_device(ng, nm, state, film_mask, basis, sample_cells, owner):
    modes, snaps = basis.shape[1], state.shape[1]
    nrow, ncol = state.shape[2:]
    samp = sample_cells.shape[1]
    nchunk = 2 * nrow
    width = 2 * nm * (modes + snaps)
    dma = pltpu.SemaphoreType.DMA
    vmem = pl.BlockSpec(memory_space=pltpu.VMEM)
    hbm = pl.BlockSpec(memory_space=pl.ANY)
    outs = pl.pallas_call(
        functools.partial(kernel, ng, nm, nrow * ncol / samp),
        out_shape=(
            pltpu.VMEM((nm * modes // ng, snaps), F32),
            pltpu.VMEM((1, ng * 8, width), BF16),
            pltpu.VMEM((2, nm * modes), F32),
            pltpu.VMEM((2, nm * snaps), F32),
        ),
        in_specs=[hbm] * 5,
        out_specs=(vmem, vmem, vmem, vmem),
        scratch_shapes=[
            pltpu.VMEM((nrow, ncol), jnp.int32),
            pltpu.VMEM((1, samp), jnp.int32),
            pltpu.VMEM((1, samp), jnp.int32),
            pltpu.VMEM((2, modes, nrow, ncol), BF16),
            pltpu.VMEM((nm // 2, 2, modes, nrow, ncol // 4), BF16),
            pltpu.VMEM((2, snaps, nrow, ncol), BF16),
            pltpu.VMEM((nrow + 2, snaps, ncol), BF16),
            pltpu.VMEM((nrow, 2 * (snaps + modes), ncol), BF16),
            pltpu.VMEM((nrow, 2 * snaps, ncol), BF16),
            pltpu.VMEM((nchunk, nm // 2, modes, ncol), BF16),
            pltpu.VMEM((ncol, samp), BF16),
            pltpu.VMEM((ng, 8 * nm, samp), BF16),
            pltpu.VMEM((2 * (snaps + modes), samp), F32),
            pltpu.VMEM((2 * (snaps + modes), samp), BF16),
            pltpu.VMEM((2, nm, modes, samp), BF16),
            pltpu.VMEM((ng, 8 * nm, 2 * snaps), BF16),
            pltpu.VMEM((ng, 8 * nm, 2 * snaps), BF16),
            pltpu.VMEM((nm, 8 * ng, 2 * snaps), BF16),
            pltpu.VMEM((nm, 8 * ng, 2 * snaps), BF16),
            pltpu.VMEM((2, 128, 2 * snaps), BF16),
            pltpu.VMEM((ng, 16, nm * modes), F32),
            pltpu.VMEM((ng, 16, nm * modes), BF16),
            pltpu.VMEM((ng, 16, nm * modes), BF16),
            pltpu.VMEM((ng, 16, 256), F32),
            pltpu.VMEM((ng, 16, 256), F32),
            pltpu.VMEM((nm, 8, 256), F32),
            pltpu.VMEM((nm, 8, 256), F32),
            pltpu.VMEM((3 * modes, 2 * snaps), F32),
            pltpu.VMEM((modes, 2 * snaps), F32),
            pltpu.VMEM((2, nm // 2, 2, nm * modes // ng, snaps), F32),
            pltpu.VMEM((ng, nm * modes // ng, snaps), F32),
            dma((8,)),
            dma((7, nchunk + 4)),
            dma((4, 2, nchunk + 4)),
            dma((4,)),
            dma((2, nm + 2)),
            dma((2, ng)),
            dma((2, ng)),
            dma((2, ng)),
            dma((2, nm)),
            dma((2, ng)),
            dma((2, nrow)),
            pltpu.SemaphoreType.REGULAR((3,)),
        ],
        compiler_params=pltpu.CompilerParams(
            collective_id=0, has_side_effects=True, vmem_limit_bytes=59 << 20
        ),
    )(state, basis, film_mask, sample_cells, owner.reshape(1, samp))
    return pl.pallas_call(
        finish,
        out_shape=tuple(jax.ShapeDtypeStruct(o.shape, o.dtype) for o in outs),
        in_specs=[vmem] * 4,
        out_specs=(vmem,) * 4,
    )(*[pltpu.with_memory_space_constraint(o, pltpu.VMEM) for o in outs])


def solution(mesh):
    in_specs = (
        P(None, "mode", "grid", None),
        P("grid", None),
        P(None, "mode", "grid", None),
        P("grid", None),
        P("grid", None, None),
    )
    out_specs = (
        P("grid", "mode"),
        P(("grid", "mode"), None, None),
        P(("grid", "mode"), None),
        P(("grid", "mode"), None),
    )
    return jax.shard_map(
        functools.partial(per_device, mesh.shape["grid"], mesh.shape["mode"]),
        mesh=mesh, in_specs=in_specs, out_specs=out_specs, check_vma=False,
    )
```
